32 devices in a mesh: dp: 4 (over x, core), ctx: 8 (over z, y).
Axes of the slice: x: 2, y: 2, z: 4, core: 2. Of those that a mesh axis runs over, the one named last changes fastest.
Arguments:
- tokens: bfloat16 [4, 1024, 768], P('dp', 'ctx'), may hold values from -6 to 6
- segment_numbers: int32 [4, 1024], P('dp', 'ctx'), may hold values from 0 to 7, as said below
- cotangent: bfloat16 [4, 1024, 768], P('dp', 'ctx'), may hold values from -6 to 6
- query_key_value_weight: bfloat16 [768, 2304], P(('dp', 'ctx')), may hold values from -0.21875 to 0.21875
- query_key_value_bias: bfloat16 [2304], P(('dp', 'ctx')), may hold values from -3 to 3
- output_matrix: bfloat16 [768, 768], P(('dp', 'ctx')), may hold values from -1.75 to 1.75
- output_bias: bfloat16 [768], P(('dp', 'ctx')), may hold values from -2 to 2
- up_matrix: bfloat16 [768, 3072], P(('dp', 'ctx')), may hold values from -0.21875 to 0.21875
- up_input_bias: bfloat16 [3072], P(('dp', 'ctx')), may hold values from -3 to 3
- down_matrix: bfloat16 [3072, 768], P(('dp', 'ctx')), may hold values from -0.109375 to 0.109375
- down_output_bias: bfloat16 [768], P(('dp', 'ctx')), may hold values from -2 to 2
- first_gain: bfloat16 [768], P(('dp', 'ctx')), may hold values from 0.099609375 to 1.8984375
- first_shift: bfloat16 [768], P(('dp', 'ctx')), may hold values from -2 to 2
- second_gain: bfloat16 [768], P(('dp', 'ctx')), may hold values from 0.099609375 to 1.8984375
- second_shift: bfloat16 [768], P(('dp', 'ctx')), may hold values from -2 to 2
Outputs:
- mixed: bfloat16 [4, 1024, 768], P('dp', 'ctx')
- tokens_grad: bfloat16 [4, 1024, 768], P('dp', 'ctx')
- qkv_weight_grad: float32 [768, 2304], P(('dp', 'ctx'))
- qkv_bias_grad: float32 [2304], P(('dp', 'ctx'))
- out_weight_grad: float32 [768, 768], P(('dp', 'ctx'))
- out_bias_grad: float32 [768], P(('dp', 'ctx'))
- up_weight_grad: float32 [768, 3072], P(('dp', 'ctx'))
- up_bias_grad: float32 [3072], P(('dp', 'ctx'))
- down_weight_grad: float32 [3072, 768], P(('dp', 'ctx'))
- down_bias_grad: float32 [768], P(('dp', 'ctx'))
- first_gain_grad: float32 [768], P(('dp', 'ctx'))
- first_shift_grad: float32 [768], P(('dp', 'ctx'))
- second_gain_grad: float32 [768], P(('dp', 'ctx'))
- second_shift_grad: float32 [768], P(('dp', 'ctx'))
The draws below stay inside these ranges and needn't reach their ends.
Inputs may be any that keep to these rules, and one draw needn't show every extreme that they name: `segment_numbers`: within each sequence the numbers start at 0 and never fall, each number marking one document of consecutive tokens. The sequences of the even indices of dp hold exactly 3 documents. In such a sequence the first document ends within its first 128 tokens and the last starts within its last 128 tokens. Every other sequence holds exactly 8 documents.
All inputs are finite; a program needn't handle non-finite values.
Results may differ from the reference program's by a relative error of at most 0.0099.
Values may be sent and summed in bfloat16 or wider, within the bound.
No kernel may reach another device: no remote copies, remote signals or barrier semaphores. Data moves between devices by JAX's collectives and lax.ppermute only.
A program may use at most 192 MiB of HBM per device.

```python
import math
import jax
import jax.numpy as jnp
from jax import lax

D = 768
H = 12
HD = 64
ROT = 16
FF = 3072
BLK = 128
SEQS = 1
SEQ_ALL = 4
SEQUENCE_TOKENS = 1024


def boundary_row(key):
    order = jax.random.permutation(key, SEQUENCE_TOKENS - 1).astype(jnp.int32)
    column = jnp.arange(SEQUENCE_TOKENS, dtype=jnp.int32)
    chosen = order[:7] + 1
    return jnp.any(column[:, None] == chosen[None, :], axis=1)


def draw_segment_numbers(key, part):
    key = jax.random.fold_in(key, 11)
    first, second, third, fourth = jax.random.split(key, 4)
    row_keys = jax.random.split(first, SEQ_ALL)
    fresh = jax.vmap(boundary_row)(row_keys)
    groups = SEQ_ALL // SEQS
    pick = jax.random.randint(second, (groups,), 0, SEQS)
    rows = jnp.arange(SEQ_ALL, dtype=jnp.int32)
    group_of = rows // SEQS
    chosen_group = jnp.logical_or(jnp.full((SEQ_ALL,), SEQS > 1), group_of % 2 == 0)
    single = (rows % SEQS == pick[group_of]) & chosen_group
    early = jax.random.randint(third, (groups,), 1, BLK).astype(jnp.int32)
    late = (SEQUENCE_TOKENS - BLK + jax.random.randint(fourth, (groups,), 1, BLK)).astype(jnp.int32)
    column = jnp.arange(SEQUENCE_TOKENS, dtype=jnp.int32)
    ends = (column[None, :] == early[group_of][:, None]) | (column[None, :] == late[group_of][:, None])
    fresh = jnp.where(single[:, None], ends, fresh)
    return jnp.cumsum(fresh.astype(jnp.int32), axis=1).astype(jnp.int32)


def with_spikes(values, key, source, target, shards_of, factor):
    def block_of(dim):
        return (jnp.arange(values.shape[dim]) // (values.shape[dim] // shards_of)).reshape((-1,) + (1,) * (values.ndim - 1 - dim))

    first = jax.random.permutation(key, shards_of)[block_of(target)]
    second = (block_of(target) + shards_of // 2) % shards_of
    return jnp.where((block_of(source) == first) | (block_of(source) == second), factor * values, values)


def levels(rng, shape, cuts, low, high):
    def one(dim, shards_of):
        draws = jax.random.uniform(jax.random.fold_in(jax.random.fold_in(rng, 6), dim), (shards_of,), jnp.float32, low / len(cuts), high / len(cuts))
        return jnp.repeat(jnp.exp(draws), shape[dim] // shards_of).reshape((-1,) + (1,) * (len(shape) - dim - 1))

    level = one(*cuts[0])
    for cut in cuts[1:]:
        level = level * one(*cut)
    return level


def centred(own_key, shape, deviation, bound, pieces=(), kind=jnp.bfloat16):
    drawn = jax.random.normal(own_key, shape, jnp.float32) * deviation
    if len(pieces) > 0:
        drawn = levels(own_key, shape, pieces, -0.22, 0.18) * drawn
    return jnp.clip(drawn, min=-bound, max=bound).astype(kind)


def bell_draw_with(stream_key, shape, scale, bound, pieces, heavy, held_as=jnp.bfloat16):
    entries = scale * jax.random.normal(stream_key, shape, jnp.float32)
    if pieces:
        entries = entries * levels(stream_key, shape, pieces, -0.22, 0.18)
    return jnp.clip(with_spikes(entries, jax.random.fold_in(stream_key, 3), *heavy), -bound, bound).astype(held_as)


def setup_inputs(seed: int = 0) -> dict:
    splits = jax.random.split(jax.random.key(seed), 16)
    return {
        "tokens": bell_draw_with(splits[0], (SEQ_ALL, SEQUENCE_TOKENS, D), 1.0, 6.0, ((0, 4), (1, 8)), (1, 2, 8, 2.0)),
        "segment_numbers": draw_segment_numbers(jax.random.fold_in(splits[15], 71), 0),
        "cotangent": centred(splits[2], (SEQ_ALL, SEQUENCE_TOKENS, D), 1.0, 6.0, ((0, 4), (1, 8))),
        "query_key_value_weight": centred(splits[3], (D, 3 * D), D ** -0.5, 0.21875, ((0, 32),)),
        "query_key_value_bias": centred(splits[4], (3 * D,), 0.5, 3.0, ((0, 32),)),
        "output_matrix": centred(splits[5], (D, D), (max(16 * D // SEQUENCE_TOKENS, 1)) ** -0.5, 1.75, ((0, 32),)),
        "output_bias": centred(splits[6], (D,), 0.3, 2.0, ((0, 32),)),
        "up_matrix": centred(splits[7], (D, FF), D ** -0.5, 0.21875, ((0, 32),)),
        "up_input_bias": centred(splits[8], (FF,), 0.5, 3.0, ((0, 32),)),
        "down_matrix": centred(splits[9], (FF, D), FF ** -0.5, 0.109375, ((0, 32),)),
        "down_output_bias": centred(splits[10], (D,), 0.3, 2.0, ((0, 32),)),
        "first_gain": jnp.clip(1.0 + 0.18 * jax.random.normal(splits[11], (D,), jnp.float32), 0.099609375, 1.8984375).astype(jnp.bfloat16),
        "first_shift": centred(splits[12], (D,), 0.3, 2.0, ((0, 32),)),
        "second_gain": jnp.clip(1.0 + 0.18 * jax.random.normal(splits[13], (D,), jnp.float32), 0.099609375, 1.8984375).astype(jnp.bfloat16),
        "second_shift": centred(splits[14], (D,), 0.3, 2.0, ((0, 32),)),
    }


@jax.custom_vjp
def low(v):
    return lax.optimization_barrier(v.astype(jnp.bfloat16)).astype(jnp.float32)

@jax.custom_vjp
def lowered_backward(v):
    return v

def low_keep(v):
    return (low(v), None)

def low_pass(kept, grad):
    return (grad,)

def back_keep(v):
    return (v, None)

def back_low(kept, grad):
    return (low(grad),)
low.defvjp(low_keep, low_pass)
lowered_backward.defvjp(back_keep, back_low)
eps = 1e-05
highest_precision = lax.Precision.HIGHEST

def doc_positions(segment_numbers):
    index = jnp.arange(SEQUENCE_TOKENS, dtype=jnp.int32)
    fresh = jnp.concatenate([jnp.ones((segment_numbers.shape[0], 1), jnp.bool_), segment_numbers[:, 1:] != segment_numbers[:, :-1]], axis=1)
    starts = lax.cummax(jnp.where(fresh, index[None, :], jnp.zeros_like(segment_numbers)), axis=1)
    return (index[None, :] - starts).astype(jnp.int32)

def rotate(field, position):
    half = ROT // 2
    freq = 10000.0 ** (-jnp.arange(half, dtype=jnp.float32) * 2.0 / ROT)
    angle = position.astype(jnp.float32)[..., None] * freq
    cosine = jnp.cos(angle)[..., None, :]
    sine = jnp.sin(angle)[..., None, :]
    first = field[..., :half]
    second = field[..., half:ROT]
    return jnp.concatenate([first * cosine - second * sine, second * cosine + first * sine, field[..., ROT:]], axis=-1)

def attend_rows(query_portion, index_portion, score_portion, key, value_rows, segment_row):
    score_matrix = jnp.einsum('qhd,khd->hqk', query_portion, key, precision=highest_precision) * HD ** (-0.5)
    score_matrix = lowered_backward(score_matrix)
    key_index = jnp.arange(SEQUENCE_TOKENS, dtype=jnp.int32)
    allowed_pairs = (key_index[None, :] <= index_portion[:, None]) & (segment_row[None, :] == score_portion[:, None])
    score_matrix = jnp.where(allowed_pairs[None], score_matrix, -1e+30)
    weights = low(jax.nn.softmax(score_matrix, axis=-1))
    return jnp.einsum('hqk,khd->qhd', weights, value_rows, precision=highest_precision)

def attend_sequence(items):
    query_rows, key, value_rows, segment_row = items
    block_length = math.gcd(SEQUENCE_TOKENS, 512)
    token_count = SEQUENCE_TOKENS // block_length
    index = jnp.arange(SEQUENCE_TOKENS, dtype=jnp.int32)

    def one_block(block):
        query_portion, index_portion, score_portion = block
        return attend_rows(query_portion, index_portion, score_portion, key, value_rows, segment_row)
    out = lax.map(jax.checkpoint(one_block), (query_rows.reshape(token_count, block_length, H, HD), index.reshape(token_count, block_length), segment_row.reshape(token_count, block_length)))
    return out.reshape(SEQUENCE_TOKENS, H, HD)

def layer(tokens, query_key_value_weight, query_key_value_bias, output_matrix, output_bias, up_matrix, up_input_bias, down_matrix, down_output_bias, first_gain, first_shift, second_gain, second_shift, position, segment_numbers):
    mean = lax.optimization_barrier(jnp.mean(tokens, axis=-1, keepdims=True))
    centered = tokens - mean
    normed = centered * lax.rsqrt(lax.optimization_barrier(jnp.mean(centered * centered, axis=-1, keepdims=True)) + eps)
    first_input = low(normed * first_gain + first_shift)
    second_input = low(normed * second_gain + second_shift)
    query_key_value = lowered_backward(jnp.einsum('vpu,ui->vpi', first_input, query_key_value_weight, precision=highest_precision) + query_key_value_bias)
    query_rows = low(rotate(query_key_value[..., :D].reshape(SEQ_ALL, SEQUENCE_TOKENS, H, HD), position))
    key = low(rotate(query_key_value[..., D:2 * D].reshape(SEQ_ALL, SEQUENCE_TOKENS, H, HD), position))
    value_rows = low(query_key_value[..., 2 * D:].reshape(SEQ_ALL, SEQUENCE_TOKENS, H, HD))
    attended_output = lax.map(jax.checkpoint(attend_sequence), (query_rows, key, value_rows, segment_numbers))
    attended_output = lowered_backward(low(attended_output.reshape(SEQ_ALL, SEQUENCE_TOKENS, D)))
    attention_block = jnp.einsum('vpu,ui->vpi', attended_output, output_matrix, precision=highest_precision) + output_bias
    pre_activation = lowered_backward(jnp.einsum('zrm,mq->zrq', second_input, up_matrix, precision=highest_precision) + up_input_bias)
    hidden_state = low(jax.nn.gelu(pre_activation, approximate=False))
    feed_forward = jnp.einsum('cae,et->cat', hidden_state, down_matrix, precision=highest_precision) + down_output_bias
    return tokens + attention_block + feed_forward

def reference(tokens, segment_numbers, cotangent, query_key_value_weight, query_key_value_bias, output_matrix, output_bias, up_matrix, up_input_bias, down_matrix, down_output_bias, first_gain, first_shift, second_gain, second_shift):
    position = doc_positions(segment_numbers)
    primal = [a.astype(jnp.float32) for a in (tokens, query_key_value_weight, query_key_value_bias, output_matrix, output_bias, up_matrix, up_input_bias, down_matrix, down_output_bias, first_gain, first_shift, second_gain, second_shift)]

    def forward(*params):
        return layer(*params, position, segment_numbers)
    mixed, pullback = jax.vjp(forward, *primal)
    grads = pullback(cotangent.astype(jnp.float32))
    return (mixed.astype(jnp.bfloat16), grads[0].astype(jnp.bfloat16), grads[1].astype(jnp.float32), grads[2].astype(jnp.float32), grads[3].astype(jnp.float32), grads[4].astype(jnp.float32), grads[5].astype(jnp.float32), grads[6].astype(jnp.float32), grads[7].astype(jnp.float32), grads[8].astype(jnp.float32), grads[9].astype(jnp.float32), grads[10].astype(jnp.float32), grads[11].astype(jnp.float32), grads[12].astype(jnp.float32))
```

```python
from functools import partial
import math

import jax
import jax.numpy as jnp
from jax import lax
from jax.sharding import PartitionSpec as P

HD = 64
ROT = 16


eps = 1e-05


def rotation_tables(position):
    half = ROT // 2
    freq = 10000.0 ** (-jnp.arange(half, dtype=jnp.float32) * 2.0 / ROT)
    angle = position.astype(jnp.float32)[..., None] * freq
    return (jnp.cos(angle)[..., None, :], jnp.sin(angle)[..., None, :])


def rotate(field, cosine, sine):
    half = ROT // 2
    first = field[..., :half]
    second = field[..., half:ROT]
    return jnp.concatenate(
        [first * cosine - second * sine, second * cosine + first * sine, field[..., ROT:]], axis=-1
    )


def rotate_back(grad, cosine, sine):
    half = ROT // 2
    first = grad[..., :half]
    second = grad[..., half:ROT]
    return jnp.concatenate(
        [first * cosine + second * sine, second * cosine - first * sine, grad[..., ROT:]], axis=-1
    )


def over_blocks(step, carry, piece, start_offset):
    width = piece[0].shape[1]
    block_length = math.gcd(width, 512)
    token_count = width // block_length

    def advance(number, state):
        offset = number * block_length
        part = tuple((lax.dynamic_slice_in_dim(p, offset, block_length, 1) for p in piece))
        return step(state, part, start_offset + offset)

    return lax.fori_loop(0, token_count, advance, carry)


def scores_masked(query_rows, key, query_index, query_segment, key_index, key_segment):
    seqs, width = (key.shape[0], key.shape[1])
    keys = key.reshape(seqs, width, query_rows.shape[2], HD)
    score_matrix = jnp.einsum(
        "sqhd,skhd->shqk", query_rows, keys, preferred_element_type=jnp.float32
    ) * HD ** (-0.5)
    allowed_pairs = (key_index[None, None, :] <= query_index[None, :, None]) & (
        key_segment[:, None, :] == query_segment[:, :, None]
    )
    return (score_matrix, allowed_pairs[:, None])


def gathered_plan(
    tokens,
    segment_numbers,
    cotangent,
    query_key_value_weight,
    query_key_value_bias,
    output_matrix,
    output_bias,
    up_matrix,
    up_input_bias,
    down_matrix,
    down_output_bias,
    first_gain,
    first_shift,
    second_gain,
    second_shift,
):
    seqs, block, width = tokens.shape
    heads = width // HD
    rows = seqs * block
    scale = HD ** (-0.5)
    w_qkv, b_qkv, w_out, b_out, w_up, b_up, w_down, b_down, g_one, s_one, g_two, s_two = (
        lax.all_gather(query_key_value_weight, ("dp", "ctx"), axis=0, tiled=True),
        lax.all_gather(query_key_value_bias, ("dp", "ctx"), axis=0, tiled=True),
        lax.all_gather(output_matrix, ("dp", "ctx"), axis=0, tiled=True),
        lax.all_gather(output_bias, ("dp", "ctx"), axis=0, tiled=True),
        lax.all_gather(up_matrix, ("dp", "ctx"), axis=0, tiled=True),
        lax.all_gather(up_input_bias, ("dp", "ctx"), axis=0, tiled=True),
        lax.all_gather(down_matrix, ("dp", "ctx"), axis=0, tiled=True),
        lax.all_gather(down_output_bias, ("dp", "ctx"), axis=0, tiled=True),
        lax.all_gather(first_gain, ("dp", "ctx"), axis=0, tiled=True),
        lax.all_gather(first_shift, ("dp", "ctx"), axis=0, tiled=True),
        lax.all_gather(second_gain, ("dp", "ctx"), axis=0, tiled=True),
        lax.all_gather(second_shift, ("dp", "ctx"), axis=0, tiled=True),
    )
    seg_all = lax.all_gather(segment_numbers, "ctx", axis=1, tiled=True)
    length = seg_all.shape[1]
    index_all = jnp.arange(length, dtype=jnp.int32)
    fresh = jnp.concatenate(
        [jnp.ones((seqs, 1), jnp.bool_), seg_all[:, 1:] != seg_all[:, :-1]], axis=1
    )
    starts = lax.cummax(jnp.where(fresh, index_all[None, :], jnp.zeros_like(seg_all)), axis=1)
    offset = lax.axis_index("ctx") * block
    query_index = offset + jnp.arange(block, dtype=jnp.int32)
    position = query_index[None, :] - lax.dynamic_slice_in_dim(starts, offset, block, 1)
    cosine, sine = rotation_tables(position)
    xval = tokens.reshape(rows, width).astype(jnp.float32)
    mean = jnp.mean(xval, axis=-1, keepdims=True)
    centered = xval - mean
    inverse = lax.rsqrt(jnp.mean(centered * centered, axis=-1, keepdims=True) + eps)
    normed = centered * inverse
    first_input = (normed * g_one.astype(jnp.float32) + s_one.astype(jnp.float32)).astype(
        jnp.bfloat16
    )
    second_input = (normed * g_two.astype(jnp.float32) + s_two.astype(jnp.float32)).astype(
        jnp.bfloat16
    )
    query_key_value = jnp.dot(
        first_input, w_qkv, preferred_element_type=jnp.float32
    ) + b_qkv.astype(jnp.float32)
    query_key_value = query_key_value.reshape(seqs, block, 3 * width)
    query_block = rotate(
        query_key_value[..., :width].reshape(seqs, block, heads, HD), cosine, sine
    ).astype(jnp.bfloat16)
    key_b = (
        rotate(
            query_key_value[..., width : 2 * width].reshape(seqs, block, heads, HD), cosine, sine
        )
        .astype(jnp.bfloat16)
        .reshape(seqs, block, width)
    )
    value_b = query_key_value[..., 2 * width :].astype(jnp.bfloat16)

    def forward_step(carry, piece, start_offset):
        top, total, acc = carry
        key, value_rows = piece
        token_count = key.shape[1]
        key_index = start_offset + jnp.arange(token_count, dtype=jnp.int32)
        key_segment = lax.dynamic_slice_in_dim(seg_all, start_offset, token_count, 1)
        score_matrix, allowed_pairs = scores_masked(
            query_block, key, query_index, segment_numbers, key_index, key_segment
        )
        masked = jnp.where(allowed_pairs, score_matrix, -1e30)
        new_top = jnp.maximum(top, jnp.max(masked, axis=-1))
        weights = jnp.where(allowed_pairs, jnp.exp(masked - new_top[..., None]), 0.0)
        decay = jnp.exp(top - new_top)
        values = value_rows.reshape(seqs, token_count, heads, HD)
        total = total * decay + jnp.sum(weights, axis=-1)
        acc = acc * decay[..., None] + jnp.einsum(
            "shqk,skhd->shqd",
            weights.astype(jnp.bfloat16),
            values,
            preferred_element_type=jnp.float32,
        )
        return (new_top, total, acc)

    init = (
        jnp.full((seqs, heads, block), -1e30, jnp.float32),
        jnp.zeros((seqs, heads, block), jnp.float32),
        jnp.zeros((seqs, heads, block, HD), jnp.float32),
    )
    top, total, acc = over_blocks(
        forward_step,
        init,
        (
            lax.all_gather(key_b, "ctx", axis=1, tiled=True),
            lax.all_gather(value_b, "ctx", axis=1, tiled=True),
        ),
        jnp.int32(0),
    )
    attended_output = acc / total[..., None]
    log_sum_exp = top + jnp.log(total)
    attended_rows = attended_output.transpose(0, 2, 1, 3).reshape(rows, width)
    attended_b = attended_rows.astype(jnp.bfloat16)
    attention_block = jnp.dot(attended_b, w_out, preferred_element_type=jnp.float32) + b_out.astype(
        jnp.float32
    )
    pre_activation = jnp.dot(second_input, w_up, preferred_element_type=jnp.float32) + b_up.astype(
        jnp.float32
    )
    hidden_state, gelu_back = jax.vjp(partial(jax.nn.gelu, approximate=False), pre_activation)
    hidden_b = hidden_state.astype(jnp.bfloat16)
    feed_forward = jnp.dot(hidden_b, w_down, preferred_element_type=jnp.float32) + b_down.astype(
        jnp.float32
    )
    mixed = (xval + attention_block + feed_forward).astype(jnp.bfloat16).reshape(seqs, block, width)
    v_qkv, v_out, v_up, v_down, h_one, h_two = (
        lax.all_gather(query_key_value_weight, ("dp", "ctx"), axis=0, tiled=True),
        lax.all_gather(output_matrix, ("dp", "ctx"), axis=0, tiled=True),
        lax.all_gather(up_matrix, ("dp", "ctx"), axis=0, tiled=True),
        lax.all_gather(down_matrix, ("dp", "ctx"), axis=0, tiled=True),
        lax.all_gather(first_gain, ("dp", "ctx"), axis=0, tiled=True),
        lax.all_gather(second_gain, ("dp", "ctx"), axis=0, tiled=True),
    )
    kv_all = (
        lax.all_gather(key_b, "ctx", axis=1, tiled=True),
        lax.all_gather(value_b, "ctx", axis=1, tiled=True),
    )
    cot_b = cotangent.reshape(rows, width)
    cot = cot_b.astype(jnp.float32)
    grad_down_w = jnp.dot(hidden_b.T, cot_b, preferred_element_type=jnp.float32)
    grad_down_b = jnp.sum(cot, axis=0)
    grad_out_w = jnp.dot(attended_b.T, cot_b, preferred_element_type=jnp.float32)
    hidden_grad = jnp.dot(cot_b, v_down.T, preferred_element_type=jnp.float32)
    pre_grad = gelu_back(hidden_grad)[0].astype(jnp.bfloat16)
    grad_up_w = jnp.dot(second_input.T, pre_grad, preferred_element_type=jnp.float32)
    grad_up_b = jnp.sum(pre_grad.astype(jnp.float32), axis=0)
    second_grad = jnp.dot(pre_grad, v_up.T, preferred_element_type=jnp.float32)
    attended_grad = jnp.dot(cot_b, v_out.T, preferred_element_type=jnp.float32).astype(jnp.bfloat16)
    output_gradient_block = attended_grad.reshape(seqs, block, heads, HD)
    outgrad_f = output_gradient_block.astype(jnp.float32)
    delta_terms = jnp.sum(outgrad_f.transpose(0, 2, 1, 3) * attended_output, axis=-1)

    def pair_gradients(
        query_portion,
        gradient_portion,
        logsum_portion,
        delta_portion,
        query_position,
        query_segment,
        key,
        value_rows,
        key_index,
        key_segment,
    ):
        token_count = key.shape[1]
        score_matrix, allowed_pairs = scores_masked(
            query_portion, key, query_position, query_segment, key_index, key_segment
        )
        weights = jnp.where(allowed_pairs, jnp.exp(score_matrix - logsum_portion[..., None]), 0.0)
        values = value_rows.reshape(seqs, token_count, heads, HD)
        prob_grad = jnp.einsum(
            "sqhd,skhd->shqk", gradient_portion, values, preferred_element_type=jnp.float32
        )
        score_grad = (weights * (prob_grad - delta_portion[..., None])).astype(jnp.bfloat16)
        return (weights, score_grad)

    def query_step(carry, piece, start_offset):
        key, value_rows = piece
        token_count = key.shape[1]
        key_index = start_offset + jnp.arange(token_count, dtype=jnp.int32)
        key_segment = lax.dynamic_slice_in_dim(seg_all, start_offset, token_count, 1)
        weights, score_grad = pair_gradients(
            query_block,
            output_gradient_block,
            log_sum_exp,
            delta_terms,
            query_index,
            segment_numbers,
            key,
            value_rows,
            key_index,
            key_segment,
        )
        keys = key.reshape(seqs, token_count, heads, HD)
        return (
            carry
            + jnp.einsum("shqk,skhd->shqd", score_grad, keys, preferred_element_type=jnp.float32)
            * scale
        )

    query_grad = over_blocks(
        query_step, jnp.zeros((seqs, heads, block, HD), jnp.float32), kv_all, 0
    )
    token_count = block * lax.axis_size("ctx")
    block_length = math.gcd(token_count, 512)

    def one_block(number):
        begin_offset = number * block_length
        key = lax.dynamic_slice_in_dim(kv_all[0], begin_offset, block_length, 1)
        value_rows = lax.dynamic_slice_in_dim(kv_all[1], begin_offset, block_length, 1)
        key_index = begin_offset + jnp.arange(block_length, dtype=jnp.int32)
        key_segment = lax.dynamic_slice_in_dim(seg_all, begin_offset, block_length, 1)
        weights, score_grad = pair_gradients(
            query_block,
            output_gradient_block,
            log_sum_exp,
            delta_terms,
            query_index,
            segment_numbers,
            key,
            value_rows,
            key_index,
            key_segment,
        )
        key_grad = (
            jnp.einsum(
                "shqk,sqhd->skhd", score_grad, query_block, preferred_element_type=jnp.float32
            )
            * scale
        )
        value_grad = jnp.einsum(
            "shqk,sqhd->skhd",
            weights.astype(jnp.bfloat16),
            output_gradient_block,
            preferred_element_type=jnp.float32,
        )
        paired = jnp.concatenate(
            [
                key_grad.reshape(seqs, block_length, width),
                value_grad.reshape(seqs, block_length, width),
            ],
            axis=-1,
        )
        return paired.transpose(1, 0, 2)

    parts = lax.map(one_block, jnp.arange(token_count // block_length, dtype=jnp.int32))
    kv_grad = lax.psum_scatter(
        parts.reshape(token_count, seqs, 2 * width), "ctx", scatter_dimension=0, tiled=True
    ).transpose(1, 0, 2)
    query_back = rotate_back(query_grad.transpose(0, 2, 1, 3), cosine, sine).reshape(
        seqs, block, width
    )
    key_back = rotate_back(
        kv_grad[..., :width].reshape(seqs, block, heads, HD), cosine, sine
    ).reshape(seqs, block, width)
    qkv_grad = (
        jnp.concatenate([query_back, key_back, kv_grad[..., width:]], axis=-1)
        .reshape(rows, 3 * width)
        .astype(jnp.bfloat16)
    )
    grad_qkv_w = jnp.dot(first_input.T, qkv_grad, preferred_element_type=jnp.float32)
    grad_qkv_b = jnp.sum(qkv_grad.astype(jnp.float32), axis=0)
    first_grad = jnp.dot(qkv_grad, v_qkv.T, preferred_element_type=jnp.float32)
    grad_g_one = jnp.sum(normed * first_grad, axis=0)
    grad_s_one = jnp.sum(first_grad, axis=0)
    grad_g_two = jnp.sum(normed * second_grad, axis=0)
    grad_s_two = jnp.sum(second_grad, axis=0)
    normed_grad = first_grad * h_one.astype(jnp.float32) + second_grad * h_two.astype(jnp.float32)
    inner = (
        normed_grad
        - jnp.mean(normed_grad, axis=-1, keepdims=True)
        - normed * jnp.mean(normed_grad * normed, axis=-1, keepdims=True)
    )
    tokens_grad = (cot + inner * inverse).astype(jnp.bfloat16).reshape(seqs, block, width)
    shards = (
        lax.psum_scatter(grad_qkv_w, ("dp", "ctx"), scatter_dimension=0, tiled=True),
        lax.psum_scatter(grad_qkv_b, ("dp", "ctx"), scatter_dimension=0, tiled=True),
        lax.psum_scatter(grad_out_w, ("dp", "ctx"), scatter_dimension=0, tiled=True),
        lax.psum_scatter(grad_down_b, ("dp", "ctx"), scatter_dimension=0, tiled=True),
        lax.psum_scatter(grad_up_w, ("dp", "ctx"), scatter_dimension=0, tiled=True),
        lax.psum_scatter(grad_up_b, ("dp", "ctx"), scatter_dimension=0, tiled=True),
        lax.psum_scatter(grad_down_w, ("dp", "ctx"), scatter_dimension=0, tiled=True),
        lax.psum_scatter(grad_down_b, ("dp", "ctx"), scatter_dimension=0, tiled=True),
        lax.psum_scatter(grad_g_one, ("dp", "ctx"), scatter_dimension=0, tiled=True),
        lax.psum_scatter(grad_s_one, ("dp", "ctx"), scatter_dimension=0, tiled=True),
        lax.psum_scatter(grad_g_two, ("dp", "ctx"), scatter_dimension=0, tiled=True),
        lax.psum_scatter(grad_s_two, ("dp", "ctx"), scatter_dimension=0, tiled=True),
    )
    return (mixed, tokens_grad) + tuple(shards)


def swapped(x, bit):
    size = lax.axis_size("ctx")
    return lax.ppermute(x, "ctx", [(i, i ^ bit) for i in range(size)])


def slot_order(size):
    return list(range(0, size, 2)) + list(range(1, size, 2))


def gather_slots(x):
    size = lax.axis_size("ctx")
    near = jnp.stack([x] + [swapped(x, bit) for bit in range(2, size, 2)])
    return jnp.concatenate([near, swapped(near, 1)], axis=0)


def reduce_slots(parts):
    size = lax.axis_size("ctx")
    half = size // 2
    near = parts[:half].astype(jnp.float32) + swapped(parts[half:], 1).astype(jnp.float32)
    low = near.astype(jnp.bfloat16)
    total = near[0]
    for number in range(1, half):
        total = total + swapped(low[number], 2 * number).astype(jnp.float32)
    return total


def between(x, offset, mine):
    nd, nc = lax.axis_size("dp"), lax.axis_size("ctx")
    pairs = []
    for d in range(nd):
        step = offset if mine is None else mine[d]
        pairs += [
            (d * nc + c + step, d * nc + c) for c in range(nc) if 0 <= c + step < nc
        ]
    return lax.ppermute(x, ("dp", "ctx"), pairs)


def split_low(x):
    high = x.astype(jnp.bfloat16)
    return high, (x - high.astype(jnp.float32)).astype(jnp.bfloat16)


def head_split_plan(
    tokens,
    segment_numbers,
    cotangent,
    query_key_value_weight,
    query_key_value_bias,
    output_matrix,
    output_bias,
    up_matrix,
    up_input_bias,
    down_matrix,
    down_output_bias,
    first_gain,
    first_shift,
    second_gain,
    second_shift,
):
    f32, bf16 = jnp.float32, jnp.bfloat16
    nd, nc = lax.axis_size("dp"), lax.axis_size("ctx")
    block, width = tokens.shape[1], tokens.shape[2]
    heads = width // HD
    per_d = heads // nd
    held = nd // 2
    rows = query_key_value_weight.shape[0]
    units = down_matrix.shape[0]
    ff = nd * units
    cols = held * HD
    length = nc * block
    d, c = lax.axis_index("dp"), lax.axis_index("ctx")
    group = c // 3
    half = c % 3
    active = half < 2
    half_in = jnp.minimum(half, 1)
    order = jnp.asarray(slot_order(nc), jnp.int32)
    blocks = c ^ order

    qkv_parts = query_key_value_weight.reshape(rows, 3, 2, held, per_d, HD).transpose(4, 2, 0, 1, 3, 5)
    qkv_parts = qkv_parts.reshape(per_d, 2, rows, 3 * cols)
    qkv_parts = jnp.concatenate([qkv_parts, jnp.zeros_like(qkv_parts[:, :1])], axis=1)
    qkv_parts = qkv_parts.reshape(3 * per_d, rows, 3 * cols)[:nc]
    up_parts = up_matrix.reshape(rows, nd, nc, units).transpose(2, 0, 1, 3).reshape(nc, rows, ff)
    vector = jnp.concatenate(
        [
            query_key_value_bias,
            up_input_bias,
            output_bias,
            down_output_bias,
            first_gain,
            first_shift,
            second_gain,
            second_shift,
            segment_numbers.reshape(block).astype(bf16),
        ]
    )
    vector = jnp.pad(vector, (0, width - vector.shape[0]))
    message = jnp.concatenate([qkv_parts, up_parts], axis=-1)
    message = jnp.concatenate(
        [message, jnp.broadcast_to(jnp.pad(vector[None], ((0, 7), (0, 0)))[None], (nc, 8, width))], axis=1
    )
    x_all = gather_slots(tokens[0]).reshape(length, width)
    arrived = lax.all_to_all(message, "ctx", 0, 0, tiled=True)
    two = [2 if k < nd // 2 else -2 for k in range(nd)]
    after = between(output_matrix, 1, None)
    before = between(output_matrix, -1, None)
    far = between(output_matrix, 0, two)
    strip = jnp.concatenate([far, before, output_matrix, after, far], axis=0)
    in_lower = d < nd // 2
    target = jnp.where(in_lower, half == 0, half == 1)
    begin = HD * group - rows * (c - 2)
    begin = jnp.where(target, begin, 0)
    out_slot = lax.dynamic_slice_in_dim(strip, begin, HD, 0)
    package = jnp.concatenate(
        [arrived[:, :rows].reshape(nc * rows, width), down_matrix, out_slot, arrived[:, rows]], axis=0
    )
    every = lax.all_gather(package, "dp", axis=0, tiled=False)
    n1 = nc * rows
    n2 = n1 + units
    n3 = n2 + HD
    w_qkv = every[:, :n1, : 3 * cols].reshape(width, 3 * cols)
    w_up = every[:, :n1, 3 * cols :].reshape(width, ff)
    w_down = every[:, n1:n2].reshape(ff, width)
    w_out = lax.dynamic_slice_in_dim(every[:, n2:n3], held * half_in, held, 0).reshape(cols, width)
    vectors = every[:, n3:].reshape(nd * nc, width)
    nb = query_key_value_bias.shape[0]
    nu = up_input_bias.shape[0]
    b_qkv = vectors[:, :nb].reshape(3, 2, held, per_d, HD)
    b_qkv = lax.dynamic_index_in_dim(b_qkv, half_in, 1, False)
    b_qkv = lax.dynamic_index_in_dim(b_qkv, group, 2, False).reshape(3 * cols)
    b_qkv = jnp.where(active, b_qkv, 0).astype(f32)
    b_up = lax.dynamic_index_in_dim(vectors[:, nb : nb + nu].reshape(nd, nc, nu), c, 1, False).reshape(ff).astype(f32)
    at = nb + nu
    b_out, b_down, g_one, s_one, g_two, s_two = (
        vectors[:, at + k * rows : at + (k + 1) * rows].reshape(width).astype(f32) for k in range(6)
    )
    at = at + 6 * rows
    seg = lax.dynamic_slice_in_dim(vectors[:, at : at + block], d * nc, nc, 0)
    seg = jnp.take(seg, blocks, axis=0).reshape(length).astype(f32)
    index = (blocks[:, None] * block + jnp.arange(block, dtype=jnp.int32)[None, :]).reshape(length)
    start = jnp.sum((seg[None, :] < seg[:, None]).astype(f32), axis=1)
    position = index.astype(f32) - start
    cosine, sine = rotation_tables(position)

    xval = x_all.astype(f32)
    mean = jnp.mean(xval, axis=-1, keepdims=True)
    centered = xval - mean
    inverse = lax.rsqrt(jnp.mean(centered * centered, axis=-1, keepdims=True) + eps)
    normed = centered * inverse
    first_input = (normed * g_one + s_one).astype(bf16)
    second_input = (normed * g_two + s_two).astype(bf16)
    qkv = jnp.dot(first_input, w_qkv, preferred_element_type=f32) + b_qkv
    qkv = qkv.reshape(length, 3, held, HD)
    query = rotate(qkv[:, 0], cosine, sine).astype(bf16)
    key = rotate(qkv[:, 1], cosine, sine).astype(bf16)
    value = qkv[:, 2].astype(bf16)
    scale = HD ** (-0.5)
    allowed = (index[None, :] <= index[:, None]) & (seg[None, :] == seg[:, None])
    scores = jnp.einsum("qhd,khd->hqk", query, key, preferred_element_type=f32) * scale
    scores = jnp.where(allowed[None], scores, -1e30)
    top = jnp.max(scores, axis=-1, keepdims=True)
    weights = jnp.exp(scores - top)
    weights = weights / jnp.sum(weights, axis=-1, keepdims=True)
    weights_low = weights.astype(bf16)
    attended = jnp.einsum("hqk,khd->qhd", weights_low, value, preferred_element_type=f32)
    attended_low = attended.astype(bf16).reshape(length, cols)
    pre = jnp.dot(second_input, w_up, preferred_element_type=f32) + b_up
    hidden, gelu_back = jax.vjp(partial(jax.nn.gelu, approximate=False), pre)
    hidden_low = hidden.astype(bf16)
    mixed_part = jnp.dot(attended_low, w_out, preferred_element_type=f32) + jnp.dot(
        hidden_low, w_down, preferred_element_type=f32
    )
    mixed_sum = reduce_slots(mixed_part.astype(bf16).reshape(nc, block, width))
    mixed = (tokens[0].astype(f32) + (mixed_sum + (b_out + b_down))).astype(bf16)

    g_all = gather_slots(cotangent[0]).reshape(length, width)
    own = cotangent[0].astype(f32)
    grad_down_w = jnp.dot(hidden_low.T, g_all, preferred_element_type=f32)
    grad_out_w = jnp.dot(attended_low.T, g_all, preferred_element_type=f32)
    hidden_grad = jnp.dot(g_all, w_down.T, preferred_element_type=f32)
    pre_grad = gelu_back(hidden_grad)[0].astype(bf16)
    grad_up_w = jnp.dot(second_input.T, pre_grad, preferred_element_type=f32)
    grad_up_b = jnp.sum(pre_grad.astype(f32), axis=0)
    second_grad = jnp.dot(pre_grad, w_up.T, preferred_element_type=f32)
    attended_grad = jnp.dot(g_all, w_out.T, preferred_element_type=f32).astype(bf16).reshape(length, held, HD)
    delta = jnp.sum(attended_grad.astype(f32) * attended, axis=-1)
    prob_grad = jnp.einsum("qhd,khd->hqk", attended_grad, value, preferred_element_type=f32)
    score_grad = (weights * (prob_grad - delta.T[:, :, None])).astype(bf16)
    query_grad = jnp.einsum("hqk,khd->qhd", score_grad, key, preferred_element_type=f32) * scale
    key_grad = jnp.einsum("hqk,qhd->khd", score_grad, query, preferred_element_type=f32) * scale
    value_grad = jnp.einsum("hqk,qhd->khd", weights_low, attended_grad, preferred_element_type=f32)
    qkv_grad = jnp.stack(
        [rotate_back(query_grad, cosine, sine), rotate_back(key_grad, cosine, sine), value_grad], axis=1
    ).astype(bf16)
    qkv_grad = qkv_grad.reshape(length, 3 * cols)
    grad_qkv_w = jnp.dot(first_input.T, qkv_grad, preferred_element_type=f32)
    grad_qkv_b = jnp.sum(qkv_grad.astype(f32), axis=0)
    first_grad = jnp.dot(qkv_grad, w_qkv.T, preferred_element_type=f32)
    inner_part = first_grad * g_one + second_grad * g_two
    inner_sum = reduce_slots(inner_part.astype(bf16).reshape(nc, block, width))
    own_x = tokens[0].astype(f32)
    own_centered = own_x - jnp.mean(own_x, axis=-1, keepdims=True)
    own_inverse = lax.rsqrt(jnp.mean(own_centered * own_centered, axis=-1, keepdims=True) + eps)
    own_normed = own_centered * own_inverse
    inner = (
        inner_sum
        - jnp.mean(inner_sum, axis=-1, keepdims=True)
        - own_normed * jnp.mean(inner_sum * own_normed, axis=-1, keepdims=True)
    )
    tokens_grad = (own + inner * own_inverse).astype(bf16)

    zero = jnp.zeros((), f32)
    place = jnp.zeros((3, 2, held, per_d, HD), f32)
    place = lax.dynamic_update_slice(
        place,
        jnp.where(active, grad_qkv_b, 0).reshape(3, 1, held, 1, HD),
        (0, half_in, 0, group, 0),
    ).reshape(nd, nc, nb)
    place_up = lax.dynamic_update_slice(
        jnp.zeros((nd, nc, nu), f32), grad_up_b.reshape(nd, 1, nu), (0, c, 0)
    )
    sums = [
        jnp.sum(own, axis=0),
        jnp.sum(normed * first_grad, axis=0),
        jnp.sum(first_grad, axis=0),
        jnp.sum(normed * second_grad, axis=0),
        jnp.sum(second_grad, axis=0),
    ]
    vector_grad = jnp.concatenate([place, place_up] + [s.reshape(nd, nc, rows) for s in sums], axis=-1)
    nv = vector_grad.shape[-1]

    def to_rows(values):
        high, low = split_low(values)
        both = jnp.concatenate([high, low], axis=-1)
        return jnp.pad(both, [(0, 0)] * (both.ndim - 1) + [(0, width - 2 * nv)])

    def from_rows(values):
        return values[..., :nv].astype(f32) + values[..., nv : 2 * nv].astype(f32)

    out_slots = jnp.zeros((nd, HD, width), bf16)
    out_slots = lax.dynamic_update_slice(
        out_slots,
        jnp.where(active, grad_out_w, 0).astype(bf16).reshape(held, HD, width),
        (held * half_in, 0, 0),
    )
    grads = jnp.concatenate(
        [
            jnp.concatenate([grad_qkv_w.astype(bf16), grad_up_w.astype(bf16)], axis=-1).reshape(nd, n1, width),
            grad_down_w.astype(bf16).reshape(nd, units, width),
            out_slots,
            to_rows(vector_grad),
        ],
        axis=1,
    )
    summed = jnp.sum(lax.all_to_all(grads, "dp", 0, 0, tiled=True).astype(f32), axis=0)
    down_weight_grad = summed[n1:n2]
    head_rows = jnp.where(target, summed[n2:n3], 0)
    strip_grad = lax.dynamic_update_slice(jnp.zeros((5 * rows, width), f32), head_rows, (begin, 0))
    strip_grad = strip_grad.astype(bf16).reshape(5, rows, width)
    out_weight_grad = strip_grad[2].astype(f32)
    out_weight_grad += between(strip_grad[1], 1, None).astype(f32)
    out_weight_grad += between(strip_grad[3], -1, None).astype(f32)
    out_weight_grad += between(jnp.where(in_lower, strip_grad[4], strip_grad[0]), 0, [-t for t in two]).astype(f32)
    back = jnp.concatenate(
        [
            summed[:n1].astype(bf16).reshape(nc, rows, width),
            jnp.pad(to_rows(summed[n3:, :nv] + summed[n3:, nv : 2 * nv])[:, None], ((0, 0), (0, 7), (0, 0))),
        ],
        axis=1,
    )
    back = lax.all_to_all(back, "ctx", 0, 0, tiled=True)
    qkv_back = back[:, :rows, : 3 * cols]
    qkv_back = jnp.pad(qkv_back, ((0, 3 * per_d - nc), (0, 0), (0, 0))).reshape(per_d, 3, rows, 3, held, HD)[:, :2]
    qkv_weight_grad = qkv_back.transpose(2, 3, 1, 4, 0, 5).reshape(rows, 3 * width).astype(f32)
    up_weight_grad = (
        back[:, :rows, 3 * cols :].reshape(nc, rows, nd, units).transpose(1, 2, 0, 3).reshape(rows, nc * ff).astype(f32)
    )
    vec = jnp.sum(from_rows(back[:, rows]), axis=0)
    at = nb + nu
    small = [vec[at + k * rows : at + (k + 1) * rows] for k in range(5)]
    return (
        mixed[None],
        tokens_grad[None],
        qkv_weight_grad,
        vec[:nb],
        out_weight_grad,
        small[0],
        up_weight_grad,
        vec[nb:at],
        down_weight_grad,
        small[0],
        small[1],
        small[2],
        small[3],
        small[4],
    )


def head_split_fits(nd, nc, width):
    heads = width // HD
    return nd % 2 == 0 and heads == 3 * nd and nc == 8 and width // (nd * nc) * 8 == 3 * HD


def per_device(tokens, *others):
    nd, nc = lax.axis_size("dp"), lax.axis_size("ctx")
    plan = head_split_plan if head_split_fits(nd, nc, tokens.shape[2]) else gathered_plan
    return plan(tokens, *others)


def solution(mesh):
    in_specs = (
        P("dp", "ctx", None),
        P("dp", "ctx"),
        P("dp", "ctx", None),
        P(("dp", "ctx"), None),
        P(("dp", "ctx")),
        P(("dp", "ctx"), None),
        P(("dp", "ctx")),
        P(("dp", "ctx"), None),
        P(("dp", "ctx")),
        P(("dp", "ctx"), None),
        P(("dp", "ctx")),
        P(("dp", "ctx")),
        P(("dp", "ctx")),
        P(("dp", "ctx")),
        P(("dp", "ctx")),
    )
    out_specs = (
        P("dp", "ctx", None),
        P("dp", "ctx", None),
        P(("dp", "ctx"), None),
        P(("dp", "ctx")),
        P(("dp", "ctx"), None),
        P(("dp", "ctx")),
        P(("dp", "ctx"), None),
        P(("dp", "ctx")),
        P(("dp", "ctx"), None),
        P(("dp", "ctx")),
        P(("dp", "ctx")),
        P(("dp", "ctx")),
        P(("dp", "ctx")),
        P(("dp", "ctx")),
    )
    return jax.shard_map(
        per_device, mesh=mesh, in_specs=in_specs, out_specs=out_specs, check_vma=False
    )
```

```python
from functools import partial
import math

import jax
import jax.numpy as jnp
import numpy as np
from jax import lax
from jax.experimental import pallas as pl
from jax.experimental.pallas import tpu as pltpu
from jax.sharding import PartitionSpec as P

HD = 64
ROT = 16


eps = 1e-05


def rotation_tables(position):
    half = ROT // 2
    freq = 10000.0 ** (-jnp.arange(half, dtype=jnp.float32) * 2.0 / ROT)
    angle = position.astype(jnp.float32)[..., None] * freq
    return (jnp.cos(angle)[..., None, :], jnp.sin(angle)[..., None, :])


def rotate(field, cosine, sine):
    half = ROT // 2
    first = field[..., :half]
    second = field[..., half:ROT]
    return jnp.concatenate(
        [first * cosine - second * sine, second * cosine + first * sine, field[..., ROT:]], axis=-1
    )


def rotate_back(grad, cosine, sine):
    half = ROT // 2
    first = grad[..., :half]
    second = grad[..., half:ROT]
    return jnp.concatenate(
        [first * cosine + second * sine, second * cosine - first * sine, grad[..., ROT:]], axis=-1
    )


def over_blocks(step, carry, piece, start_offset):
    width = piece[0].shape[1]
    block_length = math.gcd(width, 512)
    token_count = width // block_length

    def advance(number, state):
        offset = number * block_length
        part = tuple((lax.dynamic_slice_in_dim(p, offset, block_length, 1) for p in piece))
        return step(state, part, start_offset + offset)

    return lax.fori_loop(0, token_count, advance, carry)


def scores_masked(query_rows, key, query_index, query_segment, key_index, key_segment):
    seqs, width = (key.shape[0], key.shape[1])
    keys = key.reshape(seqs, width, query_rows.shape[2], HD)
    score_matrix = jnp.einsum(
        "sqhd,skhd->shqk", query_rows, keys, preferred_element_type=jnp.float32
    ) * HD ** (-0.5)
    allowed_pairs = (key_index[None, None, :] <= query_index[None, :, None]) & (
        key_segment[:, None, :] == query_segment[:, :, None]
    )
    return (score_matrix, allowed_pairs[:, None])


def gathered_plan(
    tokens,
    segment_numbers,
    cotangent,
    query_key_value_weight,
    query_key_value_bias,
    output_matrix,
    output_bias,
    up_matrix,
    up_input_bias,
    down_matrix,
    down_output_bias,
    first_gain,
    first_shift,
    second_gain,
    second_shift,
):
    seqs, block, width = tokens.shape
    heads = width // HD
    rows = seqs * block
    scale = HD ** (-0.5)
    w_qkv, b_qkv, w_out, b_out, w_up, b_up, w_down, b_down, g_one, s_one, g_two, s_two = (
        lax.all_gather(query_key_value_weight, ("dp", "ctx"), axis=0, tiled=True),
        lax.all_gather(query_key_value_bias, ("dp", "ctx"), axis=0, tiled=True),
        lax.all_gather(output_matrix, ("dp", "ctx"), axis=0, tiled=True),
        lax.all_gather(output_bias, ("dp", "ctx"), axis=0, tiled=True),
        lax.all_gather(up_matrix, ("dp", "ctx"), axis=0, tiled=True),
        lax.all_gather(up_input_bias, ("dp", "ctx"), axis=0, tiled=True),
        lax.all_gather(down_matrix, ("dp", "ctx"), axis=0, tiled=True),
        lax.all_gather(down_output_bias, ("dp", "ctx"), axis=0, tiled=True),
        lax.all_gather(first_gain, ("dp", "ctx"), axis=0, tiled=True),
        lax.all_gather(first_shift, ("dp", "ctx"), axis=0, tiled=True),
        lax.all_gather(second_gain, ("dp", "ctx"), axis=0, tiled=True),
        lax.all_gather(second_shift, ("dp", "ctx"), axis=0, tiled=True),
    )
    seg_all = lax.all_gather(segment_numbers, "ctx", axis=1, tiled=True)
    length = seg_all.shape[1]
    index_all = jnp.arange(length, dtype=jnp.int32)
    fresh = jnp.concatenate(
        [jnp.ones((seqs, 1), jnp.bool_), seg_all[:, 1:] != seg_all[:, :-1]], axis=1
    )
    starts = lax.cummax(jnp.where(fresh, index_all[None, :], jnp.zeros_like(seg_all)), axis=1)
    offset = lax.axis_index("ctx") * block
    query_index = offset + jnp.arange(block, dtype=jnp.int32)
    position = query_index[None, :] - lax.dynamic_slice_in_dim(starts, offset, block, 1)
    cosine, sine = rotation_tables(position)
    xval = tokens.reshape(rows, width).astype(jnp.float32)
    mean = jnp.mean(xval, axis=-1, keepdims=True)
    centered = xval - mean
    inverse = lax.rsqrt(jnp.mean(centered * centered, axis=-1, keepdims=True) + eps)
    normed = centered * inverse
    first_input = (normed * g_one.astype(jnp.float32) + s_one.astype(jnp.float32)).astype(
        jnp.bfloat16
    )
    second_input = (normed * g_two.astype(jnp.float32) + s_two.astype(jnp.float32)).astype(
        jnp.bfloat16
    )
    query_key_value = jnp.dot(
        first_input, w_qkv, preferred_element_type=jnp.float32
    ) + b_qkv.astype(jnp.float32)
    query_key_value = query_key_value.reshape(seqs, block, 3 * width)
    query_block = rotate(
        query_key_value[..., :width].reshape(seqs, block, heads, HD), cosine, sine
    ).astype(jnp.bfloat16)
    key_b = (
        rotate(
            query_key_value[..., width : 2 * width].reshape(seqs, block, heads, HD), cosine, sine
        )
        .astype(jnp.bfloat16)
        .reshape(seqs, block, width)
    )
    value_b = query_key_value[..., 2 * width :].astype(jnp.bfloat16)

    def forward_step(carry, piece, start_offset):
        top, total, acc = carry
        key, value_rows = piece
        token_count = key.shape[1]
        key_index = start_offset + jnp.arange(token_count, dtype=jnp.int32)
        key_segment = lax.dynamic_slice_in_dim(seg_all, start_offset, token_count, 1)
        score_matrix, allowed_pairs = scores_masked(
            query_block, key, query_index, segment_numbers, key_index, key_segment
        )
        masked = jnp.where(allowed_pairs, score_matrix, -1e30)
        new_top = jnp.maximum(top, jnp.max(masked, axis=-1))
        weights = jnp.where(allowed_pairs, jnp.exp(masked - new_top[..., None]), 0.0)
        decay = jnp.exp(top - new_top)
        values = value_rows.reshape(seqs, token_count, heads, HD)
        total = total * decay + jnp.sum(weights, axis=-1)
        acc = acc * decay[..., None] + jnp.einsum(
            "shqk,skhd->shqd",
            weights.astype(jnp.bfloat16),
            values,
            preferred_element_type=jnp.float32,
        )
        return (new_top, total, acc)

    init = (
        jnp.full((seqs, heads, block), -1e30, jnp.float32),
        jnp.zeros((seqs, heads, block), jnp.float32),
        jnp.zeros((seqs, heads, block, HD), jnp.float32),
    )
    top, total, acc = over_blocks(
        forward_step,
        init,
        (
            lax.all_gather(key_b, "ctx", axis=1, tiled=True),
            lax.all_gather(value_b, "ctx", axis=1, tiled=True),
        ),
        jnp.int32(0),
    )
    attended_output = acc / total[..., None]
    log_sum_exp = top + jnp.log(total)
    attended_rows = attended_output.transpose(0, 2, 1, 3).reshape(rows, width)
    attended_b = attended_rows.astype(jnp.bfloat16)
    attention_block = jnp.dot(attended_b, w_out, preferred_element_type=jnp.float32) + b_out.astype(
        jnp.float32
    )
    pre_activation = jnp.dot(second_input, w_up, preferred_element_type=jnp.float32) + b_up.astype(
        jnp.float32
    )
    hidden_state, gelu_back = jax.vjp(partial(jax.nn.gelu, approximate=False), pre_activation)
    hidden_b = hidden_state.astype(jnp.bfloat16)
    feed_forward = jnp.dot(hidden_b, w_down, preferred_element_type=jnp.float32) + b_down.astype(
        jnp.float32
    )
    mixed = (xval + attention_block + feed_forward).astype(jnp.bfloat16).reshape(seqs, block, width)
    v_qkv, v_out, v_up, v_down, h_one, h_two = (
        lax.all_gather(query_key_value_weight, ("dp", "ctx"), axis=0, tiled=True),
        lax.all_gather(output_matrix, ("dp", "ctx"), axis=0, tiled=True),
        lax.all_gather(up_matrix, ("dp", "ctx"), axis=0, tiled=True),
        lax.all_gather(down_matrix, ("dp", "ctx"), axis=0, tiled=True),
        lax.all_gather(first_gain, ("dp", "ctx"), axis=0, tiled=True),
        lax.all_gather(second_gain, ("dp", "ctx"), axis=0, tiled=True),
    )
    kv_all = (
        lax.all_gather(key_b, "ctx", axis=1, tiled=True),
        lax.all_gather(value_b, "ctx", axis=1, tiled=True),
    )
    cot_b = cotangent.reshape(rows, width)
    cot = cot_b.astype(jnp.float32)
    grad_down_w = jnp.dot(hidden_b.T, cot_b, preferred_element_type=jnp.float32)
    grad_down_b = jnp.sum(cot, axis=0)
    grad_out_w = jnp.dot(attended_b.T, cot_b, preferred_element_type=jnp.float32)
    hidden_grad = jnp.dot(cot_b, v_down.T, preferred_element_type=jnp.float32)
    pre_grad = gelu_back(hidden_grad)[0].astype(jnp.bfloat16)
    grad_up_w = jnp.dot(second_input.T, pre_grad, preferred_element_type=jnp.float32)
    grad_up_b = jnp.sum(pre_grad.astype(jnp.float32), axis=0)
    second_grad = jnp.dot(pre_grad, v_up.T, preferred_element_type=jnp.float32)
    attended_grad = jnp.dot(cot_b, v_out.T, preferred_element_type=jnp.float32).astype(jnp.bfloat16)
    output_gradient_block = attended_grad.reshape(seqs, block, heads, HD)
    outgrad_f = output_gradient_block.astype(jnp.float32)
    delta_terms = jnp.sum(outgrad_f.transpose(0, 2, 1, 3) * attended_output, axis=-1)

    def pair_gradients(
        query_portion,
        gradient_portion,
        logsum_portion,
        delta_portion,
        query_position,
        query_segment,
        key,
        value_rows,
        key_index,
        key_segment,
    ):
        token_count = key.shape[1]
        score_matrix, allowed_pairs = scores_masked(
            query_portion, key, query_position, query_segment, key_index, key_segment
        )
        weights = jnp.where(allowed_pairs, jnp.exp(score_matrix - logsum_portion[..., None]), 0.0)
        values = value_rows.reshape(seqs, token_count, heads, HD)
        prob_grad = jnp.einsum(
            "sqhd,skhd->shqk", gradient_portion, values, preferred_element_type=jnp.float32
        )
        score_grad = (weights * (prob_grad - delta_portion[..., None])).astype(jnp.bfloat16)
        return (weights, score_grad)

    def query_step(carry, piece, start_offset):
        key, value_rows = piece
        token_count = key.shape[1]
        key_index = start_offset + jnp.arange(token_count, dtype=jnp.int32)
        key_segment = lax.dynamic_slice_in_dim(seg_all, start_offset, token_count, 1)
        weights, score_grad = pair_gradients(
            query_block,
            output_gradient_block,
            log_sum_exp,
            delta_terms,
            query_index,
            segment_numbers,
            key,
            value_rows,
            key_index,
            key_segment,
        )
        keys = key.reshape(seqs, token_count, heads, HD)
        return (
            carry
            + jnp.einsum("shqk,skhd->shqd", score_grad, keys, preferred_element_type=jnp.float32)
            * scale
        )

    query_grad = over_blocks(
        query_step, jnp.zeros((seqs, heads, block, HD), jnp.float32), kv_all, 0
    )
    token_count = block * lax.axis_size("ctx")
    block_length = math.gcd(token_count, 512)

    def one_block(number):
        begin_offset = number * block_length
        key = lax.dynamic_slice_in_dim(kv_all[0], begin_offset, block_length, 1)
        value_rows = lax.dynamic_slice_in_dim(kv_all[1], begin_offset, block_length, 1)
        key_index = begin_offset + jnp.arange(block_length, dtype=jnp.int32)
        key_segment = lax.dynamic_slice_in_dim(seg_all, begin_offset, block_length, 1)
        weights, score_grad = pair_gradients(
            query_block,
            output_gradient_block,
            log_sum_exp,
            delta_terms,
            query_index,
            segment_numbers,
            key,
            value_rows,
            key_index,
            key_segment,
        )
        key_grad = (
            jnp.einsum(
                "shqk,sqhd->skhd", score_grad, query_block, preferred_element_type=jnp.float32
            )
            * scale
        )
        value_grad = jnp.einsum(
            "shqk,sqhd->skhd",
            weights.astype(jnp.bfloat16),
            output_gradient_block,
            preferred_element_type=jnp.float32,
        )
        paired = jnp.concatenate(
            [
                key_grad.reshape(seqs, block_length, width),
                value_grad.reshape(seqs, block_length, width),
            ],
            axis=-1,
        )
        return paired.transpose(1, 0, 2)

    parts = lax.map(one_block, jnp.arange(token_count // block_length, dtype=jnp.int32))
    kv_grad = lax.psum_scatter(
        parts.reshape(token_count, seqs, 2 * width), "ctx", scatter_dimension=0, tiled=True
    ).transpose(1, 0, 2)
    query_back = rotate_back(query_grad.transpose(0, 2, 1, 3), cosine, sine).reshape(
        seqs, block, width
    )
    key_back = rotate_back(
        kv_grad[..., :width].reshape(seqs, block, heads, HD), cosine, sine
    ).reshape(seqs, block, width)
    qkv_grad = (
        jnp.concatenate([query_back, key_back, kv_grad[..., width:]], axis=-1)
        .reshape(rows, 3 * width)
        .astype(jnp.bfloat16)
    )
    grad_qkv_w = jnp.dot(first_input.T, qkv_grad, preferred_element_type=jnp.float32)
    grad_qkv_b = jnp.sum(qkv_grad.astype(jnp.float32), axis=0)
    first_grad = jnp.dot(qkv_grad, v_qkv.T, preferred_element_type=jnp.float32)
    grad_g_one = jnp.sum(normed * first_grad, axis=0)
    grad_s_one = jnp.sum(first_grad, axis=0)
    grad_g_two = jnp.sum(normed * second_grad, axis=0)
    grad_s_two = jnp.sum(second_grad, axis=0)
    normed_grad = first_grad * h_one.astype(jnp.float32) + second_grad * h_two.astype(jnp.float32)
    inner = (
        normed_grad
        - jnp.mean(normed_grad, axis=-1, keepdims=True)
        - normed * jnp.mean(normed_grad * normed, axis=-1, keepdims=True)
    )
    tokens_grad = (cot + inner * inverse).astype(jnp.bfloat16).reshape(seqs, block, width)
    shards = (
        lax.psum_scatter(grad_qkv_w, ("dp", "ctx"), scatter_dimension=0, tiled=True),
        lax.psum_scatter(grad_qkv_b, ("dp", "ctx"), scatter_dimension=0, tiled=True),
        lax.psum_scatter(grad_out_w, ("dp", "ctx"), scatter_dimension=0, tiled=True),
        lax.psum_scatter(grad_down_b, ("dp", "ctx"), scatter_dimension=0, tiled=True),
        lax.psum_scatter(grad_up_w, ("dp", "ctx"), scatter_dimension=0, tiled=True),
        lax.psum_scatter(grad_up_b, ("dp", "ctx"), scatter_dimension=0, tiled=True),
        lax.psum_scatter(grad_down_w, ("dp", "ctx"), scatter_dimension=0, tiled=True),
        lax.psum_scatter(grad_down_b, ("dp", "ctx"), scatter_dimension=0, tiled=True),
        lax.psum_scatter(grad_g_one, ("dp", "ctx"), scatter_dimension=0, tiled=True),
        lax.psum_scatter(grad_s_one, ("dp", "ctx"), scatter_dimension=0, tiled=True),
        lax.psum_scatter(grad_g_two, ("dp", "ctx"), scatter_dimension=0, tiled=True),
        lax.psum_scatter(grad_s_two, ("dp", "ctx"), scatter_dimension=0, tiled=True),
    )
    return (mixed, tokens_grad) + tuple(shards)


VMEM_LIMIT = 56 * 1024 * 1024
NT = (((1,), (1,)), ((), ()))
TN = (((0,), (0,)), ((), ()))
NN = (((1,), (0,)), ((), ()))


def mm(a, b, dims=NN):
    return lax.dot_general(a, b, dims, preferred_element_type=jnp.float32)


def vmem(count):
    return [pl.BlockSpec(memory_space=pltpu.VMEM)] * count


def call(kernel, outs, operands, scratch=(), flops=0, smem=True):
    specs = vmem(len(operands))
    if smem:
        specs[0] = pl.BlockSpec(memory_space=pltpu.SMEM)
    size = sum(math.prod(o.shape) * o.dtype.itemsize for o in list(outs) + list(operands))
    return pl.pallas_call(
        kernel,
        out_shape=[jax.ShapeDtypeStruct(o.shape, o.dtype) for o in outs],
        in_specs=specs,
        out_specs=vmem(len(outs)),
        scratch_shapes=list(scratch),
        compiler_params=pltpu.CompilerParams(vmem_limit_bytes=VMEM_LIMIT),
        cost_estimate=pl.CostEstimate(flops=flops, bytes_accessed=size, transcendentals=0),
    )(*operands)


def like(shape, dtype):
    return jax.ShapeDtypeStruct(shape, dtype)


def slot_order(size):
    return list(range(0, size, 2)) + list(range(1, size, 2))


def swapped(x, bit):
    size = lax.axis_size("ctx")
    return lax.ppermute(x, "ctx", [(i, i ^ bit) for i in range(size)])


def gather_slots(x):
    size = lax.axis_size("ctx")
    near = jnp.stack([x] + [swapped(x, bit) for bit in range(2, size, 2)])
    return near, swapped(near, 1)


def reduce_slots(near, far):
    near = near.astype(jnp.float32) + swapped(far, 1).astype(jnp.float32)
    low = near.astype(jnp.bfloat16)
    total = near[0]
    for number in range(1, near.shape[0]):
        total = total + swapped(low[number], 2 * number).astype(jnp.float32)
    return total


def between(x, offset):
    nd, nc = lax.axis_size("dp"), lax.axis_size("ctx")
    pairs = [
        (d * nc + c + offset[d], d * nc + c)
        for d in range(nd)
        for c in range(nc)
        if 0 <= c + offset[d] < nc
    ]
    return lax.ppermute(x, ("dp", "ctx"), pairs)


def iota(shape, dim):
    return lax.broadcasted_iota(jnp.int32, shape, dim)


def message_kernel(per_d, nd, nc, units, qkv, up, vectors, out):
    f32 = jnp.float32
    rows = qkv.shape[0]
    width = qkv.shape[1] // 3
    held = nd // 2
    w = qkv[...].astype(f32)
    u = up[...].astype(f32)
    v = vectors[...].astype(f32)
    for t in range(nc):
        group, half = t // 3, t % 3
        pieces = []
        for part in range(3):
            for k in range(held):
                at = part * width + HD * (per_d * (held * half + k) + group)
                pieces.append(w[:, at : at + HD] if half < 2 else jnp.zeros((rows, HD), f32))
        for k in range(nd):
            at = k * nc * units + t * units
            pieces.append(u[:, at : at + units])
        out[t] = jnp.concatenate(pieces + [v], axis=1).astype(out.dtype)


def tables_kernel(arrived, freq, cosine, sine, begin):
    f32 = jnp.float32
    nc, rows, lanes = arrived.shape
    block = 128
    head = arrived[:, :, lanes - block :].astype(f32)
    seg = jnp.sum(jnp.where(iota((nc, rows, block), 1) == 8, head, 0.0), axis=1)
    row = jnp.concatenate([seg[b : b + 1] for b in range(nc)], axis=1)
    eye = iota((block, block), 0) == iota((block, block), 1)
    feature = iota((block, block), 1) % HD
    for b in range(nc):
        col = jnp.sum(jnp.where(eye, seg[b : b + 1], 0.0), axis=1, keepdims=True)
        start = jnp.sum(jnp.where(row < col, 1.0, 0.0), axis=1, keepdims=True)
        index = (iota((block, 1), 0) + b * block).astype(f32)
        angle = (index - start) * freq[...]
        at = pl.ds(b * block, block)
        cosine[at, :] = jnp.where(feature < ROT, jnp.cos(angle), 1.0)
        sign = jnp.where(feature < ROT // 2, -1.0, jnp.where(feature < ROT, 1.0, 0.0))
        sine[at, :] = sign * jnp.sin(angle)
        begin[at, :] = jnp.broadcast_to(start, (block, block))


def turned(t, cosine, sine):
    lanes = t.shape[1]
    early = iota(t.shape, 1) % HD < ROT // 2
    other = jnp.where(early, pltpu.roll(t, lanes - ROT // 2, 1), pltpu.roll(t, ROT // 2, 1))
    return t * cosine + other * sine


def allowed_pairs(begin, first_row, rows, keys):
    key_index = iota((rows, keys), 1)
    query_index = iota((rows, keys), 0) + first_row
    return (key_index <= query_index) & (key_index >= begin.astype(jnp.int32))


def head_lanes(shape, h):
    lane = iota(shape, 1)
    return (lane >= h * HD) & (lane < (h + 1) * HD)


def column_places(meta, nb, cols, width, per_d, held):
    j = iota((1, 3 * cols), 1)
    part = jnp.where(j >= 2 * cols, 2, jnp.where(j >= cols, 1, 0))
    rest = j - part * cols
    hh = jnp.zeros_like(rest)
    for k in range(1, held):
        hh = hh + jnp.where(rest >= k * HD, 1, 0)
    column = part * width + hh * (per_d * HD) + (rest - hh * HD)
    column = column + HD * (per_d * held * meta[8] + meta[9])
    owner = jnp.floor((column.astype(jnp.float32) + 0.5) / nb).astype(jnp.int32)
    return owner, column - owner * nb


def forward_kernel(
    sizes, meta, near, far, every, down, outs, cosine, sine, begin, own24, pick24, own96, pick96,
    part_near, part_far, first_in, second_in, normed, query, key, value, attended, stats, hidden, slope, vecs,
):
    f32, bf16 = jnp.float32, jnp.bfloat16
    nd, nc, per_d, held, nb, rows = sizes
    block, width = near.shape[1], near.shape[2]
    cols = held * HD
    ff = down.shape[0]
    length = nc * block
    total = nd * nc
    packed = every[:, :, 3 * cols + ff :].astype(f32).reshape(total, rows, block)
    kind = iota(packed.shape, 1)

    def of_kind(k):
        return jnp.sum(jnp.where(kind == k, packed, 0.0), axis=1).astype(bf16)

    owner = iota((total, width), 0)
    kept = owner == own24[...]
    flat = []
    for k in range(2, 8):
        flat.append(jnp.sum(jnp.where(kept, mm(of_kind(k), pick24[...]), 0.0), axis=0, keepdims=True))
    out_bias, g_one, s_one, g_two, s_two = flat[0] + flat[1], flat[2], flat[3], flat[4], flat[5]
    up_owner = iota((total, ff), 0) == own96[...] * nc + meta[10]
    b_up = jnp.sum(jnp.where(up_owner, mm(of_kind(1), pick96[...]), 0.0), axis=0, keepdims=True)
    col_owner, col_place = column_places(meta, nb, cols, width, per_d, held)
    col_pick = (iota((block, 3 * cols), 0) == col_place).astype(f32).astype(bf16)
    b_qkv = jnp.where(iota((total, 3 * cols), 0) == col_owner, mm(of_kind(0), col_pick), 0.0)
    b_qkv = jnp.sum(b_qkv, axis=0, keepdims=True) * meta[11].astype(f32)
    for k, vector in enumerate((g_one, s_one, g_two, s_two, out_bias)):
        vecs[k : k + 1, :] = vector
    for i in range(nc):
        half = near if i < nc // 2 else far
        x = half[i % (nc // 2)].astype(f32)
        centered = x - jnp.mean(x, axis=1, keepdims=True)
        n = centered * lax.rsqrt(jnp.mean(centered * centered, axis=1, keepdims=True) + eps)
        at = pl.ds(pl.multiple_of(meta[i] * block, block), block)
        normed[at, :] = n.astype(bf16)
        first_in[at, :] = (n * g_one + s_one).astype(bf16)
        second_in[at, :] = (n * g_two + s_two).astype(bf16)
    w_qkv = every[:, :, : 3 * cols].reshape(width, 3 * cols)
    w_up = every[:, :, 3 * cols : 3 * cols + ff].reshape(width, ff)
    step = 2 * block
    for b in range(length // step):
        at = pl.ds(b * step, step)
        t = mm(first_in[at, :], w_qkv) + b_qkv
        query[at, :] = (turned(t[:, :cols], cosine[at, :], sine[at, :])).astype(bf16)
        key[at, :] = turned(t[:, cols : 2 * cols], cosine[at, :], sine[at, :]).astype(bf16)
        value[at, :] = t[:, 2 * cols :].astype(bf16)
    for b in range(length // step):
        at = pl.ds(b * step, step)
        pre = mm(second_in[at, :], w_up) + b_up
        cdf = 0.5 + 0.5 * lax.erf(pre * (0.5**0.5))
        hidden[at, :] = (pre * cdf).astype(bf16)
        slope[at, :] = (cdf + pre * jnp.exp(-0.5 * pre * pre) * ((2 * math.pi) ** -0.5)).astype(bf16)
    for b in range(length // step):
        at = pl.ds(b * step, step)
        keys = (b + 1) * step
        allowed = allowed_pairs(begin[at, 0:1], b * step, step, keys)
        q = query[at, :]
        result = jnp.zeros((step, cols), f32)
        for h in range(held):
            mine = head_lanes((step, cols), h)
            s = mm(jnp.where(mine, q, jnp.zeros_like(q)), key[:keys, :], NT) * (HD**-0.5)
            s = jnp.where(allowed, s, -1e30)
            top = jnp.max(s, axis=1, keepdims=True)
            p = jnp.exp(s - top)
            inverse = 1.0 / jnp.sum(p, axis=1, keepdims=True)
            result = jnp.where(mine, mm((p * inverse).astype(bf16), value[:keys, :]), result)
            stats[at, 2 * h : 2 * h + 1] = top
            stats[at, 2 * h + 1 : 2 * h + 2] = inverse
        attended[at, :] = result
    w_out = outs[pl.ds(held * meta[8], held)].reshape(cols, width)
    for i in range(nc):
        half = part_near if i < nc // 2 else part_far
        at = pl.ds(pl.multiple_of(meta[i] * block, block), block)
        part = mm(attended[at, :].astype(bf16), w_out) + mm(hidden[at, :], down[...])
        half[i % (nc // 2)] = part.astype(bf16)


def mlp_back_kernel(
    sizes, meta, near, far, every, down, attended, hidden, slope, second_in, normed, vecs,
    grads, part, g_all, sums, pre_grad,
):
    f32, bf16 = jnp.float32, jnp.bfloat16
    nd, nc, per_d, held, nb, rows = sizes
    block, width = near.shape[1], near.shape[2]
    cols = held * HD
    ff = down.shape[0]
    length = nc * block
    for i in range(nc):
        half = near if i < nc // 2 else far
        g_all[pl.ds(pl.multiple_of(meta[i] * block, block), block), :] = half[i % (nc // 2)]
    g = g_all[...]
    rows_d = width // nd
    units = ff // nd
    side = width // 2
    grad_down = mm(hidden[...], g, TN).astype(bf16)
    for d in range(nd):
        piece = grad_down[d * units : (d + 1) * units]
        grads[d, rows_d : rows_d + units, :] = piece[:, :side]
        grads[d, rows_d + units : rows_d + 2 * units, :] = piece[:, side:]
    grad_out = mm(attended[...].astype(bf16), g, TN)
    base = rows_d + 2 * units
    for d in range(nd):
        here = (meta[8] == d // held) & (meta[11] == 1)
        k = d % held
        piece = jnp.where(here, grad_out[k * HD : (k + 1) * HD], 0.0).astype(bf16)
        grads[d, base : base + HD, :] = piece[:, :side]
        grads[d, base + HD : base + 2 * HD, :] = piece[:, side:]
    step = 2 * block
    w_up = every[:, :, 3 * cols : 3 * cols + ff].reshape(width, ff)
    g_two = vecs[2:3, :]
    up_sum = jnp.zeros((1, ff), f32)
    gain_sum = jnp.zeros((1, width), f32)
    shift_sum = jnp.zeros((1, width), f32)
    for b in range(length // step):
        at = pl.ds(b * step, step)
        back = (mm(g_all[at, :], down[...], NT) * slope[at, :].astype(f32)).astype(bf16)
        pre_grad[at, :] = back
        up_sum += jnp.sum(back.astype(f32), axis=0, keepdims=True)
        second = mm(back, w_up, NT)
        gain_sum += jnp.sum(second * normed[at, :].astype(f32), axis=0, keepdims=True)
        shift_sum += jnp.sum(second, axis=0, keepdims=True)
        part[at, :] = (second * g_two).astype(bf16)
    sums[0:1, :] = gain_sum
    sums[1:2, :] = shift_sum
    sums[2:3, :ff] = up_sum
    grad_up = mm(second_in[...], pre_grad[...], TN).astype(bf16)
    for d in range(nd):
        grads[d, :rows_d, :] = grad_up[d * rows_d : (d + 1) * rows_d]


def attention_back_kernel(
    sizes, meta, g_all, every, outs, cosine, sine, begin, query, key, value, attended, stats, first_in, normed, vecs,
    part, sums, own24, pick24, own96, pick96,
    grads, part_near, part_far, d_out, d_query, d_key, d_value, d_qkv, first_grad,
):
    f32, bf16 = jnp.float32, jnp.bfloat16
    nd, nc, per_d, held, nb, rows = sizes
    length, width = g_all.shape
    block = length // nc
    cols = held * HD
    ff = own96.shape[1]
    total = nd * nc
    w_out = outs[pl.ds(held * meta[8], held)].reshape(cols, width)
    w_qkv = every[:, :, : 3 * cols].reshape(width, 3 * cols)
    step = 2 * block
    scale = HD**-0.5
    d_key[...] = jnp.zeros_like(d_key)
    d_value[...] = jnp.zeros_like(d_value)
    for b in range(length // step):
        at = pl.ds(b * step, step)
        keys = (b + 1) * step
        allowed = allowed_pairs(begin[at, 0:1], b * step, step, keys)
        q = query[at, :]
        back = mm(g_all[at, :], w_out, NT).astype(bf16)
        product = back.astype(f32) * attended[at, :]
        result = jnp.zeros((step, cols), f32)
        for h in range(held):
            mine = head_lanes((step, cols), h)
            q_h = jnp.where(mine, q, jnp.zeros_like(q))
            back_h = jnp.where(mine, back, jnp.zeros_like(back))
            delta = jnp.sum(jnp.where(mine, product, 0.0), axis=1, keepdims=True)
            s = mm(q_h, key[:keys, :], NT) * scale
            p = jnp.exp(s - stats[at, 2 * h : 2 * h + 1]) * stats[at, 2 * h + 1 : 2 * h + 2]
            p = jnp.where(allowed, p, 0.0)
            d_p = mm(back_h, value[:keys, :], NT)
            d_s = (p * (d_p - delta)).astype(bf16)
            result = jnp.where(mine, mm(d_s, key[:keys, :]), result)
            d_key[:keys, :] += mm(d_s, q_h, TN)
            d_value[:keys, :] += mm(p.astype(bf16), back_h, TN)
        d_query[at, :] = result
    for b in range(length // step):
        at = pl.ds(b * step, step)
        c, s = cosine[at, :], sine[at, :]
        d_qkv[at, :cols] = turned(d_query[at, :] * scale, c, -s).astype(bf16)
        d_qkv[at, cols : 2 * cols] = turned(d_key[at, :] * scale, c, -s).astype(bf16)
        d_qkv[at, 2 * cols :] = d_value[at, :].astype(bf16)
    g_one = vecs[0:1, :]
    qkv_sum = jnp.zeros((1, 3 * cols), f32)
    gain_sum = jnp.zeros((1, width), f32)
    shift_sum = jnp.zeros((1, width), f32)
    for i in range(nc):
        half = part_near if i < nc // 2 else part_far
        at = pl.ds(pl.multiple_of(meta[i] * block, block), block)
        dq = d_qkv[at, :]
        qkv_sum += jnp.sum(dq.astype(f32), axis=0, keepdims=True)
        first = mm(dq, w_qkv, NT)
        gain_sum += jnp.sum(first * normed[at, :].astype(f32), axis=0, keepdims=True)
        shift_sum += jnp.sum(first, axis=0, keepdims=True)
        half[i % (nc // 2)] = (first * g_one + part[at, :].astype(f32)).astype(bf16)
    grad_qkv = mm(first_in[...], d_qkv[...], TN).astype(bf16)
    rows_d = width // nd
    for d in range(nd):
        grads[d, :, : 3 * cols] = grad_qkv[d * rows_d : (d + 1) * rows_d]
    own = g_all[pl.ds(pl.multiple_of(meta[0] * block, block), block), :].astype(f32)
    own_sum = jnp.sum(own, axis=0, keepdims=True)

    def halves(row):
        high = row.astype(bf16).astype(f32)
        return high, row - high

    kept = iota((total, width), 0) == own24[...]
    up_owner = iota((total, ff), 0) == own96[...] * nc + meta[10]
    col_owner, col_place = column_places(meta, nb, cols, width, per_d, held)
    col_pick = (iota((block, 3 * cols), 0) == col_place).astype(f32).astype(bf16)
    col_kept = iota((total, 3 * cols), 0) == col_owner
    kind = iota((total, rows, block), 1)
    packed = jnp.zeros((total, rows, block), f32)
    entries = [
        (qkv_sum * meta[11].astype(f32), col_kept, col_pick),
        (sums[2:3, :ff], up_owner, pick96[...]),
        (own_sum, kept, pick24[...]),
        (gain_sum, kept, pick24[...]),
        (shift_sum, kept, pick24[...]),
        (sums[0:1, :], kept, pick24[...]),
        (sums[1:2, :], kept, pick24[...]),
    ]
    for k, (vector, where, pick) in enumerate(entries):
        for n, piece in enumerate(halves(vector)):
            spread = mm(jnp.where(where, piece, 0.0).astype(bf16), pick, NT)
            packed = jnp.where(kind == k + 8 * n, spread[:, None, :], packed)
    grads[:, :, 3 * cols :] = packed.reshape(nd, rows_d, block).astype(bf16)


def unpack_kernel(per_d, nd, units, qkv, up, grad_qkv, grad_up, vector):
    f32 = jnp.float32
    nc = qkv.shape[0]
    held = nd // 2
    width = grad_qkv.shape[1] // 3
    cols = held * HD
    pieces = [None] * (3 * per_d * nd)
    ups = [None] * (nd * nc)
    total = jnp.zeros(vector.shape, f32)
    for t in range(nc):
        group, half = t // 3, t % 3
        w = qkv[t].astype(f32)
        if half < 2:
            for part in range(3):
                for k in range(held):
                    at = part * cols + k * HD
                    pieces[part * per_d * nd + per_d * (held * half + k) + group] = w[:, at : at + HD]
        total = total + w[:, 3 * cols :]
        u = up[t].astype(f32)
        for k in range(nd):
            ups[k * nc + t] = u[:, k * units : (k + 1) * units]
    grad_qkv[...] = jnp.concatenate(pieces, axis=1)
    grad_up[...] = jnp.concatenate(ups, axis=1)
    vector[...] = total


def head_split_plan(
    tokens,
    segment_numbers,
    cotangent,
    query_key_value_weight,
    query_key_value_bias,
    output_matrix,
    output_bias,
    up_matrix,
    up_input_bias,
    down_matrix,
    down_output_bias,
    first_gain,
    first_shift,
    second_gain,
    second_shift,
):
    f32, bf16, i32 = jnp.float32, jnp.bfloat16, jnp.int32
    nd, nc = lax.axis_size("dp"), lax.axis_size("ctx")
    block, width = tokens.shape[1], tokens.shape[2]
    per_d = width // HD // nd
    held = nd // 2
    cols = held * HD
    rows = query_key_value_weight.shape[0]
    units = down_matrix.shape[0]
    ff = nd * units
    nb, nu = query_key_value_bias.shape[0], up_input_bias.shape[0]
    length = nc * block
    rows_d = nc * rows
    sizes = (nd, nc, per_d, held, nb, rows)
    d, c = lax.axis_index("dp"), lax.axis_index("ctx")
    group, half = c // 3, c % 3
    half_in = jnp.minimum(half, 1)
    meta = jnp.concatenate(
        [c ^ jnp.asarray(slot_order(nc), i32), jnp.stack([half_in, group, c, (half < 2).astype(i32)]).astype(i32)]
    )
    lane = np.arange(width)
    own24 = jnp.asarray((lane // rows)[None], i32)
    pick24 = jnp.asarray(np.arange(block)[:, None] == lane[None] % rows, bf16)
    unit = np.arange(ff)
    own96 = jnp.asarray((unit // units)[None], i32)
    pick96 = jnp.asarray(np.arange(block)[:, None] == unit[None] % units, bf16)
    feature = np.arange(cols) % HD % (ROT // 2)
    freq = jnp.asarray((10000.0 ** (-feature * 2.0 / ROT))[None], f32)

    vectors = [
        query_key_value_bias, up_input_bias, output_bias, down_output_bias, first_gain, first_shift, second_gain,
        second_shift, segment_numbers.reshape(block).astype(bf16),
    ]
    vectors = jnp.stack([jnp.pad(v, (0, block - v.shape[0])) for v in vectors])
    vectors = jnp.pad(vectors, ((0, rows - vectors.shape[0]), (0, 0)))
    lanes = 3 * cols + ff + block
    (message,) = call(
        partial(message_kernel, per_d, nd, nc, units),
        [like((nc, rows, lanes), bf16)],
        [query_key_value_weight, up_matrix, vectors],
        smem=False,
    )
    arrived = lax.all_to_all(message, "ctx", 0, 0, tiled=True)
    x_near, x_far = gather_slots(tokens[0])
    every = lax.all_gather(arrived.reshape(rows_d, lanes), "dp", axis=0, tiled=False)
    w_down = lax.all_gather(down_matrix, "dp", axis=0, tiled=True)
    cosine, sine, begin = call(
        tables_kernel, [like((length, cols), f32)] * 3, [arrived, freq], smem=False
    )

    two = [2 if k < nd // 2 else -2 for k in range(nd)]
    after = between(output_matrix, [1] * nd)
    before = between(output_matrix, [-1] * nd)
    far = between(output_matrix, two)
    strip = jnp.concatenate([far, before, output_matrix, after, far], axis=0)
    in_lower = d < nd // 2
    target = jnp.where(in_lower, half == 0, half == 1)
    cut = jnp.where(target, HD * group - rows * (c - 2), 0)
    outs = lax.all_gather(lax.dynamic_slice_in_dim(strip, cut, HD, 0), "dp", axis=0, tiled=False)
    g_near, g_far = gather_slots(cotangent[0])

    full = lambda dtype: like((length, width), dtype)
    part_shape = like((nc // 2, block, width), bf16)
    (
        part_near, part_far, first_in, second_in, normed, query, key, value, attended, stats, hidden, slope, vecs,
    ) = call(
        partial(forward_kernel, sizes),
        [part_shape, part_shape, full(bf16), full(bf16), full(bf16)]
        + [like((length, cols), bf16)] * 3
        + [like((length, cols), f32), like((length, 128), f32)]
        + [like((length, ff), bf16)] * 2
        + [like((8, width), f32)],
        [meta, x_near, x_far, every, w_down, outs, cosine, sine, begin, own24, pick24, own96, pick96],
        flops=2 * length * width * (3 * cols + 2 * ff + cols) + 4 * held * length * length * HD,
    )
    mixed_sum = reduce_slots(part_near, part_far)
    mixed = (tokens[0].astype(f32) + (mixed_sum + vecs[4])).astype(bf16)
    grads_one, part, g_all, sums = call(
        partial(mlp_back_kernel, sizes),
        [like((nd, rows_d + 2 * units + 2 * HD, width // 2), bf16), full(bf16), full(bf16), like((8, width), f32)],
        [meta, g_near, g_far, every, w_down, attended, hidden, slope, second_in, normed, vecs],
        scratch=[pltpu.VMEM((length, ff), bf16)],
        flops=2 * length * width * (4 * ff + cols),
    )
    grads_one = lax.psum_scatter(grads_one, "dp", scatter_dimension=0, tiled=False)
    grads_two, n_near, n_far = call(
        partial(attention_back_kernel, sizes),
        [like((nd, rows_d, 3 * cols + block), bf16), part_shape, part_shape],
        [meta, g_all, every, outs, cosine, sine, begin, query, key, value, attended, stats, first_in, normed, vecs, part,
         sums, own24, pick24, own96, pick96],
        scratch=[pltpu.VMEM((length, cols), bf16)]
        + [pltpu.VMEM((length, cols), f32)] * 3
        + [pltpu.VMEM((length, 3 * cols), bf16), pltpu.VMEM((8, 128), f32)],
        flops=2 * length * width * (6 * cols + cols) + 10 * held * length * length * HD,
    )
    grads_two = lax.psum_scatter(grads_two, "dp", scatter_dimension=0, tiled=False)
    inner_sum = reduce_slots(n_near, n_far)
    own = cotangent[0].astype(f32)
    own_x = tokens[0].astype(f32)
    own_centered = own_x - jnp.mean(own_x, axis=-1, keepdims=True)
    own_inverse = lax.rsqrt(jnp.mean(own_centered * own_centered, axis=-1, keepdims=True) + eps)
    own_normed = own_centered * own_inverse
    inner = (
        inner_sum
        - jnp.mean(inner_sum, axis=-1, keepdims=True)
        - own_normed * jnp.mean(inner_sum * own_normed, axis=-1, keepdims=True)
    )
    tokens_grad = (own + inner * own_inverse).astype(bf16)

    up_back = lax.all_to_all(grads_one[:rows_d].reshape(nc, rows, ff), "ctx", 0, 0, tiled=True)
    at = rows_d + 2 * units
    down_weight_grad = jnp.concatenate([grads_one[rows_d : rows_d + units], grads_one[rows_d + units : at]], axis=1)
    head_rows = jnp.concatenate([grads_one[at : at + HD], grads_one[at + HD :]], axis=1)
    head_rows = jnp.where(target, head_rows, jnp.zeros_like(head_rows))
    strip_grad = lax.dynamic_update_slice(jnp.zeros((5 * rows, width), bf16), head_rows, (cut, 0))
    strip_grad = strip_grad.reshape(5, rows, width)
    out_weight_grad = (
        strip_grad[2].astype(f32)
        + between(strip_grad[1], [1] * nd).astype(f32)
        + between(strip_grad[3], [-1] * nd).astype(f32)
        + between(jnp.where(in_lower, strip_grad[4], strip_grad[0]), [-t for t in two]).astype(f32)
    )
    qkv_back = lax.all_to_all(grads_two.reshape(nc, rows, 3 * cols + block), "ctx", 0, 0, tiled=True)
    qkv_weight_grad, up_weight_grad, vec = call(
        partial(unpack_kernel, per_d, nd, units),
        [like((rows, 3 * width), f32), like((rows, nc * ff), f32), like((rows, block), f32)],
        [qkv_back, up_back],
        smem=False,
    )
    vec = vec[:7] + vec[8:15]
    small = [vec[k, :rows] for k in range(2, 7)]
    return (
        mixed[None],
        tokens_grad[None],
        qkv_weight_grad,
        vec[0, :nb],
        out_weight_grad,
        small[0],
        up_weight_grad,
        vec[1, :nu],
        down_weight_grad.astype(f32),
        small[0],
        small[1],
        small[2],
        small[3],
        small[4],
    )


def head_split_fits(nd, nc, width):
    return nd % 2 == 0 and width // HD == 3 * nd and nc == 8 and width // (nd * nc) * 8 == 3 * HD


def per_device(tokens, *others):
    nd, nc = lax.axis_size("dp"), lax.axis_size("ctx")
    plan = head_split_plan if head_split_fits(nd, nc, tokens.shape[2]) else gathered_plan
    return plan(tokens, *others)


def solution(mesh):
    in_specs = (
        P("dp", "ctx", None),
        P("dp", "ctx"),
        P("dp", "ctx", None),
        P(("dp", "ctx"), None),
        P(("dp", "ctx")),
        P(("dp", "ctx"), None),
        P(("dp", "ctx")),
        P(("dp", "ctx"), None),
        P(("dp", "ctx")),
        P(("dp", "ctx"), None),
        P(("dp", "ctx")),
        P(("dp", "ctx")),
        P(("dp", "ctx")),
        P(("dp", "ctx")),
        P(("dp", "ctx")),
    )
    out_specs = (
        P("dp", "ctx", None),
        P("dp", "ctx", None),
        P(("dp", "ctx"), None),
        P(("dp", "ctx")),
        P(("dp", "ctx"), None),
        P(("dp", "ctx")),
        P(("dp", "ctx"), None),
        P(("dp", "ctx")),
        P(("dp", "ctx"), None),
        P(("dp", "ctx")),
        P(("dp", "ctx")),
        P(("dp", "ctx")),
        P(("dp", "ctx")),
        P(("dp", "ctx")),
    )
    return jax.shard_map(
        per_device, mesh=mesh, in_specs=in_specs, out_specs=out_specs, check_vma=False
    )
```

```python
from functools import partial
import math

import jax
import jax.numpy as jnp
import numpy as np
from jax import lax
from jax.experimental import pallas as pl
from jax.experimental.pallas import tpu as pltpu
from jax.sharding import PartitionSpec as P

HD = 64
ROT = 16


eps = 1e-05


def rotation_tables(position):
    half = ROT // 2
    freq = 10000.0 ** (-jnp.arange(half, dtype=jnp.float32) * 2.0 / ROT)
    angle = position.astype(jnp.float32)[..., None] * freq
    return (jnp.cos(angle)[..., None, :], jnp.sin(angle)[..., None, :])


def rotate(field, cosine, sine):
    half = ROT // 2
    first = field[..., :half]
    second = field[..., half:ROT]
    return jnp.concatenate(
        [first * cosine - second * sine, second * cosine + first * sine, field[..., ROT:]], axis=-1
    )


def rotate_back(grad, cosine, sine):
    half = ROT // 2
    first = grad[..., :half]
    second = grad[..., half:ROT]
    return jnp.concatenate(
        [first * cosine + second * sine, second * cosine - first * sine, grad[..., ROT:]], axis=-1
    )


def over_blocks(step, carry, piece, start_offset):
    width = piece[0].shape[1]
    block_length = math.gcd(width, 512)
    token_count = width // block_length

    def advance(number, state):
        offset = number * block_length
        part = tuple((lax.dynamic_slice_in_dim(p, offset, block_length, 1) for p in piece))
        return step(state, part, start_offset + offset)

    return lax.fori_loop(0, token_count, advance, carry)


def scores_masked(query_rows, key, query_index, query_segment, key_index, key_segment):
    seqs, width = (key.shape[0], key.shape[1])
    keys = key.reshape(seqs, width, query_rows.shape[2], HD)
    score_matrix = jnp.einsum(
        "sqhd,skhd->shqk", query_rows, keys, preferred_element_type=jnp.float32
    ) * HD ** (-0.5)
    allowed_pairs = (key_index[None, None, :] <= query_index[None, :, None]) & (
        key_segment[:, None, :] == query_segment[:, :, None]
    )
    return (score_matrix, allowed_pairs[:, None])


def gathered_plan(
    tokens,
    segment_numbers,
    cotangent,
    query_key_value_weight,
    query_key_value_bias,
    output_matrix,
    output_bias,
    up_matrix,
    up_input_bias,
    down_matrix,
    down_output_bias,
    first_gain,
    first_shift,
    second_gain,
    second_shift,
):
    seqs, block, width = tokens.shape
    heads = width // HD
    rows = seqs * block
    scale = HD ** (-0.5)
    w_qkv, b_qkv, w_out, b_out, w_up, b_up, w_down, b_down, g_one, s_one, g_two, s_two = (
        lax.all_gather(query_key_value_weight, ("dp", "ctx"), axis=0, tiled=True),
        lax.all_gather(query_key_value_bias, ("dp", "ctx"), axis=0, tiled=True),
        lax.all_gather(output_matrix, ("dp", "ctx"), axis=0, tiled=True),
        lax.all_gather(output_bias, ("dp", "ctx"), axis=0, tiled=True),
        lax.all_gather(up_matrix, ("dp", "ctx"), axis=0, tiled=True),
        lax.all_gather(up_input_bias, ("dp", "ctx"), axis=0, tiled=True),
        lax.all_gather(down_matrix, ("dp", "ctx"), axis=0, tiled=True),
        lax.all_gather(down_output_bias, ("dp", "ctx"), axis=0, tiled=True),
        lax.all_gather(first_gain, ("dp", "ctx"), axis=0, tiled=True),
        lax.all_gather(first_shift, ("dp", "ctx"), axis=0, tiled=True),
        lax.all_gather(second_gain, ("dp", "ctx"), axis=0, tiled=True),
        lax.all_gather(second_shift, ("dp", "ctx"), axis=0, tiled=True),
    )
    seg_all = lax.all_gather(segment_numbers, "ctx", axis=1, tiled=True)
    length = seg_all.shape[1]
    index_all = jnp.arange(length, dtype=jnp.int32)
    fresh = jnp.concatenate(
        [jnp.ones((seqs, 1), jnp.bool_), seg_all[:, 1:] != seg_all[:, :-1]], axis=1
    )
    starts = lax.cummax(jnp.where(fresh, index_all[None, :], jnp.zeros_like(seg_all)), axis=1)
    offset = lax.axis_index("ctx") * block
    query_index = offset + jnp.arange(block, dtype=jnp.int32)
    position = query_index[None, :] - lax.dynamic_slice_in_dim(starts, offset, block, 1)
    cosine, sine = rotation_tables(position)
    xval = tokens.reshape(rows, width).astype(jnp.float32)
    mean = jnp.mean(xval, axis=-1, keepdims=True)
    centered = xval - mean
    inverse = lax.rsqrt(jnp.mean(centered * centered, axis=-1, keepdims=True) + eps)
    normed = centered * inverse
    first_input = (normed * g_one.astype(jnp.float32) + s_one.astype(jnp.float32)).astype(
        jnp.bfloat16
    )
    second_input = (normed * g_two.astype(jnp.float32) + s_two.astype(jnp.float32)).astype(
        jnp.bfloat16
    )
    query_key_value = jnp.dot(
        first_input, w_qkv, preferred_element_type=jnp.float32
    ) + b_qkv.astype(jnp.float32)
    query_key_value = query_key_value.reshape(seqs, block, 3 * width)
    query_block = rotate(
        query_key_value[..., :width].reshape(seqs, block, heads, HD), cosine, sine
    ).astype(jnp.bfloat16)
    key_b = (
        rotate(
            query_key_value[..., width : 2 * width].reshape(seqs, block, heads, HD), cosine, sine
        )
        .astype(jnp.bfloat16)
        .reshape(seqs, block, width)
    )
    value_b = query_key_value[..., 2 * width :].astype(jnp.bfloat16)

    def forward_step(carry, piece, start_offset):
        top, total, acc = carry
        key, value_rows = piece
        token_count = key.shape[1]
        key_index = start_offset + jnp.arange(token_count, dtype=jnp.int32)
        key_segment = lax.dynamic_slice_in_dim(seg_all, start_offset, token_count, 1)
        score_matrix, allowed_pairs = scores_masked(
            query_block, key, query_index, segment_numbers, key_index, key_segment
        )
        masked = jnp.where(allowed_pairs, score_matrix, -1e30)
        new_top = jnp.maximum(top, jnp.max(masked, axis=-1))
        weights = jnp.where(allowed_pairs, jnp.exp(masked - new_top[..., None]), 0.0)
        decay = jnp.exp(top - new_top)
        values = value_rows.reshape(seqs, token_count, heads, HD)
        total = total * decay + jnp.sum(weights, axis=-1)
        acc = acc * decay[..., None] + jnp.einsum(
            "shqk,skhd->shqd",
            weights.astype(jnp.bfloat16),
            values,
            preferred_element_type=jnp.float32,
        )
        return (new_top, total, acc)

    init = (
        jnp.full((seqs, heads, block), -1e30, jnp.float32),
        jnp.zeros((seqs, heads, block), jnp.float32),
        jnp.zeros((seqs, heads, block, HD), jnp.float32),
    )
    top, total, acc = over_blocks(
        forward_step,
        init,
        (
            lax.all_gather(key_b, "ctx", axis=1, tiled=True),
            lax.all_gather(value_b, "ctx", axis=1, tiled=True),
        ),
        jnp.int32(0),
    )
    attended_output = acc / total[..., None]
    log_sum_exp = top + jnp.log(total)
    attended_rows = attended_output.transpose(0, 2, 1, 3).reshape(rows, width)
    attended_b = attended_rows.astype(jnp.bfloat16)
    attention_block = jnp.dot(attended_b, w_out, preferred_element_type=jnp.float32) + b_out.astype(
        jnp.float32
    )
    pre_activation = jnp.dot(second_input, w_up, preferred_element_type=jnp.float32) + b_up.astype(
        jnp.float32
    )
    hidden_state, gelu_back = jax.vjp(partial(jax.nn.gelu, approximate=False), pre_activation)
    hidden_b = hidden_state.astype(jnp.bfloat16)
    feed_forward = jnp.dot(hidden_b, w_down, preferred_element_type=jnp.float32) + b_down.astype(
        jnp.float32
    )
    mixed = (xval + attention_block + feed_forward).astype(jnp.bfloat16).reshape(seqs, block, width)
    v_qkv, v_out, v_up, v_down, h_one, h_two = (
        lax.all_gather(query_key_value_weight, ("dp", "ctx"), axis=0, tiled=True),
        lax.all_gather(output_matrix, ("dp", "ctx"), axis=0, tiled=True),
        lax.all_gather(up_matrix, ("dp", "ctx"), axis=0, tiled=True),
        lax.all_gather(down_matrix, ("dp", "ctx"), axis=0, tiled=True),
        lax.all_gather(first_gain, ("dp", "ctx"), axis=0, tiled=True),
        lax.all_gather(second_gain, ("dp", "ctx"), axis=0, tiled=True),
    )
    kv_all = (
        lax.all_gather(key_b, "ctx", axis=1, tiled=True),
        lax.all_gather(value_b, "ctx", axis=1, tiled=True),
    )
    cot_b = cotangent.reshape(rows, width)
    cot = cot_b.astype(jnp.float32)
    grad_down_w = jnp.dot(hidden_b.T, cot_b, preferred_element_type=jnp.float32)
    grad_down_b = jnp.sum(cot, axis=0)
    grad_out_w = jnp.dot(attended_b.T, cot_b, preferred_element_type=jnp.float32)
    hidden_grad = jnp.dot(cot_b, v_down.T, preferred_element_type=jnp.float32)
    pre_grad = gelu_back(hidden_grad)[0].astype(jnp.bfloat16)
    grad_up_w = jnp.dot(second_input.T, pre_grad, preferred_element_type=jnp.float32)
    grad_up_b = jnp.sum(pre_grad.astype(jnp.float32), axis=0)
    second_grad = jnp.dot(pre_grad, v_up.T, preferred_element_type=jnp.float32)
    attended_grad = jnp.dot(cot_b, v_out.T, preferred_element_type=jnp.float32).astype(jnp.bfloat16)
    output_gradient_block = attended_grad.reshape(seqs, block, heads, HD)
    outgrad_f = output_gradient_block.astype(jnp.float32)
    delta_terms = jnp.sum(outgrad_f.transpose(0, 2, 1, 3) * attended_output, axis=-1)

    def pair_gradients(
        query_portion,
        gradient_portion,
        logsum_portion,
        delta_portion,
        query_position,
        query_segment,
        key,
        value_rows,
        key_index,
        key_segment,
    ):
        token_count = key.shape[1]
        score_matrix, allowed_pairs = scores_masked(
            query_portion, key, query_position, query_segment, key_index, key_segment
        )
        weights = jnp.where(allowed_pairs, jnp.exp(score_matrix - logsum_portion[..., None]), 0.0)
        values = value_rows.reshape(seqs, token_count, heads, HD)
        prob_grad = jnp.einsum(
            "sqhd,skhd->shqk", gradient_portion, values, preferred_element_type=jnp.float32
        )
        score_grad = (weights * (prob_grad - delta_portion[..., None])).astype(jnp.bfloat16)
        return (weights, score_grad)

    def query_step(carry, piece, start_offset):
        key, value_rows = piece
        token_count = key.shape[1]
        key_index = start_offset + jnp.arange(token_count, dtype=jnp.int32)
        key_segment = lax.dynamic_slice_in_dim(seg_all, start_offset, token_count, 1)
        weights, score_grad = pair_gradients(
            query_block,
            output_gradient_block,
            log_sum_exp,
            delta_terms,
            query_index,
            segment_numbers,
            key,
            value_rows,
            key_index,
            key_segment,
        )
        keys = key.reshape(seqs, token_count, heads, HD)
        return (
            carry
            + jnp.einsum("shqk,skhd->shqd", score_grad, keys, preferred_element_type=jnp.float32)
            * scale
        )

    query_grad = over_blocks(
        query_step, jnp.zeros((seqs, heads, block, HD), jnp.float32), kv_all, 0
    )
    token_count = block * lax.axis_size("ctx")
    block_length = math.gcd(token_count, 512)

    def one_block(number):
        begin_offset = number * block_length
        key = lax.dynamic_slice_in_dim(kv_all[0], begin_offset, block_length, 1)
        value_rows = lax.dynamic_slice_in_dim(kv_all[1], begin_offset, block_length, 1)
        key_index = begin_offset + jnp.arange(block_length, dtype=jnp.int32)
        key_segment = lax.dynamic_slice_in_dim(seg_all, begin_offset, block_length, 1)
        weights, score_grad = pair_gradients(
            query_block,
            output_gradient_block,
            log_sum_exp,
            delta_terms,
            query_index,
            segment_numbers,
            key,
            value_rows,
            key_index,
            key_segment,
        )
        key_grad = (
            jnp.einsum(
                "shqk,sqhd->skhd", score_grad, query_block, preferred_element_type=jnp.float32
            )
            * scale
        )
        value_grad = jnp.einsum(
            "shqk,sqhd->skhd",
            weights.astype(jnp.bfloat16),
            output_gradient_block,
            preferred_element_type=jnp.float32,
        )
        paired = jnp.concatenate(
            [
                key_grad.reshape(seqs, block_length, width),
                value_grad.reshape(seqs, block_length, width),
            ],
            axis=-1,
        )
        return paired.transpose(1, 0, 2)

    parts = lax.map(one_block, jnp.arange(token_count // block_length, dtype=jnp.int32))
    kv_grad = lax.psum_scatter(
        parts.reshape(token_count, seqs, 2 * width), "ctx", scatter_dimension=0, tiled=True
    ).transpose(1, 0, 2)
    query_back = rotate_back(query_grad.transpose(0, 2, 1, 3), cosine, sine).reshape(
        seqs, block, width
    )
    key_back = rotate_back(
        kv_grad[..., :width].reshape(seqs, block, heads, HD), cosine, sine
    ).reshape(seqs, block, width)
    qkv_grad = (
        jnp.concatenate([query_back, key_back, kv_grad[..., width:]], axis=-1)
        .reshape(rows, 3 * width)
        .astype(jnp.bfloat16)
    )
    grad_qkv_w = jnp.dot(first_input.T, qkv_grad, preferred_element_type=jnp.float32)
    grad_qkv_b = jnp.sum(qkv_grad.astype(jnp.float32), axis=0)
    first_grad = jnp.dot(qkv_grad, v_qkv.T, preferred_element_type=jnp.float32)
    grad_g_one = jnp.sum(normed * first_grad, axis=0)
    grad_s_one = jnp.sum(first_grad, axis=0)
    grad_g_two = jnp.sum(normed * second_grad, axis=0)
    grad_s_two = jnp.sum(second_grad, axis=0)
    normed_grad = first_grad * h_one.astype(jnp.float32) + second_grad * h_two.astype(jnp.float32)
    inner = (
        normed_grad
        - jnp.mean(normed_grad, axis=-1, keepdims=True)
        - normed * jnp.mean(normed_grad * normed, axis=-1, keepdims=True)
    )
    tokens_grad = (cot + inner * inverse).astype(jnp.bfloat16).reshape(seqs, block, width)
    shards = (
        lax.psum_scatter(grad_qkv_w, ("dp", "ctx"), scatter_dimension=0, tiled=True),
        lax.psum_scatter(grad_qkv_b, ("dp", "ctx"), scatter_dimension=0, tiled=True),
        lax.psum_scatter(grad_out_w, ("dp", "ctx"), scatter_dimension=0, tiled=True),
        lax.psum_scatter(grad_down_b, ("dp", "ctx"), scatter_dimension=0, tiled=True),
        lax.psum_scatter(grad_up_w, ("dp", "ctx"), scatter_dimension=0, tiled=True),
        lax.psum_scatter(grad_up_b, ("dp", "ctx"), scatter_dimension=0, tiled=True),
        lax.psum_scatter(grad_down_w, ("dp", "ctx"), scatter_dimension=0, tiled=True),
        lax.psum_scatter(grad_down_b, ("dp", "ctx"), scatter_dimension=0, tiled=True),
        lax.psum_scatter(grad_g_one, ("dp", "ctx"), scatter_dimension=0, tiled=True),
        lax.psum_scatter(grad_s_one, ("dp", "ctx"), scatter_dimension=0, tiled=True),
        lax.psum_scatter(grad_g_two, ("dp", "ctx"), scatter_dimension=0, tiled=True),
        lax.psum_scatter(grad_s_two, ("dp", "ctx"), scatter_dimension=0, tiled=True),
    )
    return (mixed, tokens_grad) + tuple(shards)


VMEM_LIMIT = 30 * 1024 * 1024
VMEM_MOST = 56 * 1024 * 1024
FORWARD_WORK = 10**8
BACKWARD_WORK = 10**8
NT = (((1,), (1,)), ((), ()))
TN = (((0,), (0,)), ((), ()))
NN = (((1,), (0,)), ((), ()))


def mm(a, b, dims=NN):
    return lax.dot_general(a, b, dims, preferred_element_type=jnp.float32)


HEAD_OF = (0, 1, None, 2)


def vmem(count):
    return [pl.BlockSpec(memory_space=pltpu.VMEM)] * count


def call(kernel, outs, operands, scratch=(), flops=0, smem=True, limit=VMEM_LIMIT):
    specs = vmem(len(operands))
    if smem:
        specs[0] = pl.BlockSpec(memory_space=pltpu.SMEM)
    return pl.pallas_call(
        kernel,
        out_shape=[jax.ShapeDtypeStruct(o.shape, o.dtype) for o in outs],
        in_specs=specs,
        out_specs=vmem(len(outs)),
        scratch_shapes=list(scratch),
        compiler_params=pltpu.CompilerParams(vmem_limit_bytes=limit),
        cost_estimate=pl.CostEstimate(flops=flops, bytes_accessed=1024, transcendentals=0),
    )(*operands)


def like(shape, dtype):
    return jax.ShapeDtypeStruct(shape, dtype)


def slot_order(size):
    return list(range(0, size, 2)) + list(range(1, size, 2))


def swapped(x, bit):
    size = lax.axis_size("ctx")
    return lax.ppermute(x, "ctx", [(i, i ^ bit) for i in range(size)])


def swapped_dp(x, bit):
    size = lax.axis_size("dp")
    return lax.ppermute(x, "dp", [(i, i ^ bit) for i in range(size)])


def after(x, *others):
    return lax.optimization_barrier((x,) + others)[0]


def sent(x, pairs):
    nd, nc = lax.axis_size("dp"), lax.axis_size("ctx")
    flat = [(d * nc + a, d * nc + b) for d in range(nd) for a, b in pairs(d)]
    return lax.ppermute(x, ("dp", "ctx"), flat)


def iota(shape, dim):
    return lax.broadcasted_iota(jnp.int32, shape, dim)


def message_kernel(per_d, nd, nc, units, meta, qkv, up, out_rows, *refs):
    f32 = jnp.float32
    vectors, out = refs[:-5], refs[-1]
    mine, two, four, six = refs[-5:-1]
    c = meta[10]
    rows = qkv.shape[0]
    width = qkv.shape[1] // 3
    held = nd // 2
    w = qkv[...].astype(f32)
    u = up[...].astype(f32)
    lines = []
    for vector in vectors:
        line = vector[...].astype(f32)
        if line.shape[1] < 128:
            line = jnp.concatenate([line, jnp.zeros((1, 128 - line.shape[1]), f32)], axis=1)
        lines.append(line)
    v = jnp.concatenate(lines + [jnp.zeros((rows - len(lines), 128), f32)], axis=0)
    for t in range(nc):
        group, half = HEAD_OF[t // 2], t % 2
        pieces = []
        for part in range(3):
            for k in range(held):
                at = part * width + HD * (per_d * (held * half + k) + (group or 0))
                pieces.append(jnp.zeros((rows, HD), f32) if group is None else w[:, at : at + HD])
        for k in range(nd):
            at = k * nc * units + t * units
            pieces.append(u[:, at : at + units])
        out[c ^ t] = jnp.concatenate(pieces + [v], axis=1).astype(out.dtype)
    blank = jnp.zeros((rows, out.shape[2] - width), f32)
    head = jnp.concatenate([out_rows[...].astype(f32), blank], axis=1).astype(out.dtype)
    mine[0], mine[1], mine[2] = out[0], out[1], head
    two[0], two[1], two[2] = out[2], out[3], head
    four[0], four[1] = out[4], out[5]
    six[0], six[1], six[2] = out[6], out[7], head


def package_kernel(meta, mine, two, four, six, far, down, out, natural, strip):
    f32 = jnp.float32
    nc, rows, lanes = natural.shape
    c = meta[10]
    width = down.shape[1]
    for k, near in enumerate((mine, two, four, six)):
        natural[c ^ (2 * k)] = near[0].astype(f32)
        natural[c ^ (2 * k + 1)] = far[k].astype(f32)
    out[: nc * rows, :] = natural[...].reshape(nc * rows, lanes).astype(out.dtype)
    strip[...] = jnp.zeros_like(strip)
    strip[c] = mine[2].astype(f32)
    strip[c ^ 2] = two[2].astype(f32)
    strip[c ^ 6] = six[2].astype(f32)
    strip[c ^ 1] = far[4].astype(f32)
    strip[meta[13]] = far[5].astype(f32)
    whole = strip[...].reshape(nc * rows, lanes)
    group = meta[9]
    head = jnp.where(group == 0, whole[:HD], jnp.where(group == 1, whole[HD : 2 * HD], whole[2 * HD : 3 * HD]))
    tail = jnp.concatenate([down[...].astype(f32), head[:, :width]], axis=0)
    blank = jnp.zeros((tail.shape[0], lanes - width), f32)
    out[nc * rows :, :] = jnp.concatenate([tail, blank], axis=1).astype(out.dtype)


def tables_kernel(nc, rows, package, freq, cosine, sine, begin):
    f32 = jnp.float32
    lanes = package.shape[1]
    block = 128
    head = package[: nc * rows, lanes - block :].astype(f32).reshape(nc, rows, block)
    seg = jnp.sum(jnp.where(iota((nc, rows, block), 1) == 8, head, 0.0), axis=1)
    start = jnp.zeros((nc, block), f32)
    for number in range(1, 8):
        earlier = jnp.where(seg < number, 1.0, 0.0)
        count = jnp.sum(jnp.sum(earlier, axis=1, keepdims=True), axis=0, keepdims=True)
        start = jnp.where(seg == number, count, start)
    index = (iota((nc, block), 0) * block + iota((nc, block), 1)).astype(f32)

    def as_row(x):
        return jnp.concatenate([x[b : b + 1] for b in range(nc)], axis=1)

    half = ROT // 2
    angle = freq[...] * as_row(index - start)
    table = jnp.concatenate(
        [jnp.cos(angle), jnp.sin(angle), jnp.broadcast_to(as_row(start), angle.shape)], axis=0
    )
    feature = iota((3 * half, block), 1) % HD
    row = iota((3 * half, block), 0)
    first, second = feature == row, feature == row + half
    rotary = feature < ROT
    is_first, is_second = jnp.where(first & rotary, 1.0, 0.0), jnp.where(second & rotary, 1.0, 0.0)
    pick_cos = jnp.where(row < half, is_first + is_second, 0.0)
    row2 = row - half
    sine_first = jnp.where((feature == row2) & rotary & (row2 >= 0), -1.0, 0.0)
    sine_second = jnp.where((feature == row2 + half) & rotary & (row2 >= 0), 1.0, 0.0)
    pick_sin = jnp.where(row < 2 * half, sine_first + sine_second, 0.0)
    pick_start = jnp.where(row == 2 * half, 1.0, 0.0)

    def spread(pick):
        return lax.dot_general(
            table, pick, TN, precision=lax.Precision.HIGHEST, preferred_element_type=f32
        )

    still = jnp.where(iota((1, block), 1) % HD < ROT, 0.0, 1.0)
    cosine[...] = spread(pick_cos) + still
    sine[...] = spread(pick_sin)
    begin[...] = spread(pick_start)


def turned(t, cosine, sine):
    lanes = t.shape[1]
    early = iota(t.shape, 1) % HD < ROT // 2
    other = jnp.where(early, pltpu.roll(t, lanes - ROT // 2, 1), pltpu.roll(t, ROT // 2, 1))
    return t * cosine + other * sine


def allowed_pairs(begin, first_row, rows, keys):
    key_index = iota((rows, keys), 1)
    query_index = iota((rows, keys), 0) + first_row
    return (key_index <= query_index) & (key_index >= begin.astype(jnp.int32))


def head_lanes(shape, h):
    lane = iota(shape, 1)
    return (lane >= h * HD) & (lane < (h + 1) * HD)


def column_places(meta, nb, cols, width, per_d, held):
    j = iota((1, 3 * cols), 1)
    part = jnp.where(j >= 2 * cols, 2, jnp.where(j >= cols, 1, 0))
    rest = j - part * cols
    hh = jnp.zeros_like(rest)
    for k in range(1, held):
        hh = hh + jnp.where(rest >= k * HD, 1, 0)
    column = part * width + hh * (per_d * HD) + (rest - hh * HD)
    column = column + HD * (per_d * held * meta[8] + meta[9])
    owner = jnp.floor((column.astype(jnp.float32) + 0.5) / nb).astype(jnp.int32)
    return owner, column - owner * nb


def forward_kernel(
    sizes, meta, near, far, own_pair, other_pair, cosine, sine, begin, own24, pick24, own96, pick96,
    out_near, out_far, first_in, second_in, normed, query, key, value, attended, stats, hidden, slope, vecs, weights,
    w_out, down, every, outs,
):
    f32, bf16 = jnp.float32, jnp.bfloat16
    nd, nc, per_d, held, nb, rows = sizes
    block, width = near.shape[1], near.shape[2]
    cols = held * HD
    ff = own96.shape[1]
    length = nc * block
    total = nd * nc
    n1 = nc * rows
    n2 = n1 + ff // nd
    for i, pair in enumerate((own_pair, other_pair) * 2):
        other = meta[12] ^ i
        piece = pair.at[i // 2]
        every[other] = piece[:n1]
        down[pl.ds(pl.multiple_of(other * (ff // nd), ff // nd), ff // nd), :] = piece[n1:n2, :width]
        outs[other] = piece[n2:, :width]
    w_out[...] = outs[pl.ds(held * meta[8], held)].reshape(cols, width)
    weights[...] = every[:, :, : 3 * cols + ff].reshape(width, 3 * cols + ff)
    packed = every[:, :, 3 * cols + ff :].astype(f32).reshape(total, rows, block)
    kind = iota(packed.shape, 1)

    def of_kind(k):
        return jnp.sum(jnp.where(kind == k, packed, 0.0), axis=1).astype(bf16)

    owner = iota((total, width), 0)
    kept = owner == own24[...]
    flat = []
    for k in range(2, 8):
        flat.append(jnp.sum(jnp.where(kept, mm(of_kind(k), pick24[...]), 0.0), axis=0, keepdims=True))
    out_bias, g_one, s_one, g_two, s_two = flat[0] + flat[1], flat[2], flat[3], flat[4], flat[5]
    up_owner = iota((total, ff), 0) == own96[...] * nc + meta[10]
    b_up = jnp.sum(jnp.where(up_owner, mm(of_kind(1), pick96[...]), 0.0), axis=0, keepdims=True)
    col_owner, col_place = column_places(meta, nb, cols, width, per_d, held)
    col_pick = (iota((block, 3 * cols), 0) == col_place).astype(f32).astype(bf16)
    b_qkv = jnp.where(iota((total, 3 * cols), 0) == col_owner, mm(of_kind(0), col_pick), 0.0)
    b_qkv = jnp.sum(b_qkv, axis=0, keepdims=True) * meta[11].astype(f32)
    for k, vector in enumerate((g_one, s_one, g_two, s_two, out_bias)):
        vecs[k : k + 1, :] = vector
    for i in range(nc):
        half = near if i < nc // 2 else far
        x = half[i % (nc // 2)].astype(f32)
        centered = x - jnp.mean(x, axis=1, keepdims=True)
        n = centered * lax.rsqrt(jnp.mean(centered * centered, axis=1, keepdims=True) + eps)
        at = pl.ds(pl.multiple_of(meta[i] * block, block), block)
        normed[at, :] = n.astype(bf16)
        first_in[at, :] = (n * g_one + s_one).astype(bf16)
        second_in[at, :] = (n * g_two + s_two).astype(bf16)
    w_qkv = weights[:, : 3 * cols]
    w_up = weights[:, 3 * cols :]
    step = 2 * block
    for b in range(length // step):
        at = pl.ds(b * step, step)
        t = mm(first_in[at, :], w_qkv) + b_qkv
        query[at, :] = (turned(t[:, :cols], cosine[at, :], sine[at, :])).astype(bf16)
        key[at, :] = turned(t[:, cols : 2 * cols], cosine[at, :], sine[at, :]).astype(bf16)
        value[at, :] = t[:, 2 * cols :].astype(bf16)
    for b in range(length // step):
        at = pl.ds(b * step, step)
        pre = mm(second_in[at, :], w_up) + b_up
        cdf = 0.5 + 0.5 * lax.erf(pre * (0.5**0.5))
        hidden[at, :] = (pre * cdf).astype(bf16)
        slope[at, :] = (cdf + pre * jnp.exp(-0.5 * pre * pre) * ((2 * math.pi) ** -0.5)).astype(bf16)
    for b in range(length // step):
        at = pl.ds(b * step, step)
        keys = (b + 1) * step
        allowed = allowed_pairs(begin[at, 0:1], b * step, step, keys)
        q = query[at, :]
        result = jnp.zeros((step, cols), f32)
        for h in range(held):
            mine = head_lanes((step, cols), h)
            s = mm(jnp.where(mine, q, jnp.zeros_like(q)), key[:keys, :], NT) * (HD**-0.5)
            s = jnp.where(allowed, s, -1e30)
            top = jnp.max(s, axis=1, keepdims=True)
            p = jnp.exp(s - top)
            inverse = 1.0 / jnp.sum(p, axis=1, keepdims=True)
            result = jnp.where(mine, mm((p * inverse).astype(bf16), value[:keys, :]), result)
            stats[at, 2 * h : 2 * h + 1] = top
            stats[at, 2 * h + 1 : 2 * h + 2] = inverse
        attended[at, :] = result
    for i in range(nc):
        half = out_near if i < nc // 2 else out_far
        at = pl.ds(pl.multiple_of(meta[i] * block, block), block)
        piece = mm(attended[at, :].astype(bf16), w_out[...]) + mm(hidden[at, :], down[...])
        half[i % (nc // 2)] = piece.astype(bf16)


def mlp_back(
    sizes, meta, near, far, weights, down, attended, hidden, slope, second_in, normed, vecs, part, g_all, sums, pre_grad,
    grads, place,
):
    f32, bf16 = jnp.float32, jnp.bfloat16
    nd, nc, per_d, held, nb, rows = sizes
    block, width = near.shape[1], near.shape[2]
    cols = held * HD
    ff = down.shape[0]
    units = ff // nd
    length = nc * block
    for i in range(nc):
        half = near if i < nc // 2 else far
        g_all[pl.ds(pl.multiple_of(meta[i] * block, block), block), :] = half[i % (nc // 2)]
    g = g_all[...]
    rows_d = width // nd
    side = width // 2

    grad_down = mm(hidden[...], g, TN).astype(bf16)
    for d in range(nd):
        piece = grad_down[d * units : (d + 1) * units]
        slot = place(d)
        grads[slot, rows_d : rows_d + units, :] = piece[:, :side]
        grads[slot, rows_d + units : rows_d + 2 * units, :] = piece[:, side:]
    grad_out = mm(attended[...].astype(bf16), g, TN)
    base = rows_d + 2 * units
    for d in range(nd):
        here = (meta[8] == d // held) & (meta[11] == 1)
        k = d % held
        piece = jnp.where(here, grad_out[k * HD : (k + 1) * HD], 0.0).astype(bf16)
        slot = place(d)
        grads[slot, base : base + HD, :] = piece[:, :side]
        grads[slot, base + HD : base + 2 * HD, :] = piece[:, side:]
    step = 2 * block
    w_up = weights[:, 3 * cols :]
    g_two = vecs[2:3, :]
    up_sum = jnp.zeros((1, ff), f32)
    gain_sum = jnp.zeros((1, width), f32)
    shift_sum = jnp.zeros((1, width), f32)
    for b in range(length // step):
        at = pl.ds(b * step, step)
        back = (mm(g_all[at, :], down[...], NT) * slope[at, :].astype(f32)).astype(bf16)
        pre_grad[at, :] = back
        up_sum += jnp.sum(back.astype(f32), axis=0, keepdims=True)
        second = mm(back, w_up, NT)
        gain_sum += jnp.sum(second * normed[at, :].astype(f32), axis=0, keepdims=True)
        shift_sum += jnp.sum(second, axis=0, keepdims=True)
        part[at, :] = (second * g_two).astype(bf16)
    sums[0:1, :] = gain_sum
    sums[1:2, :] = shift_sum
    sums[2:3, :ff] = up_sum
    grad_up = mm(second_in[...], pre_grad[...], TN).astype(bf16)
    for d in range(nd):
        grads[place(d), :rows_d, :] = grad_up[d * rows_d : (d + 1) * rows_d]


def attention_back(
    sizes, meta, g_all, w_out, cosine, sine, begin, query, key, value, attended, stats, d_qkv, d_query, d_key, d_value
):
    f32, bf16 = jnp.float32, jnp.bfloat16
    nd, nc, per_d, held, nb, rows = sizes
    length, width = g_all.shape
    block = length // nc
    cols = held * HD
    step = 2 * block
    scale = HD**-0.5
    d_key[...] = jnp.zeros_like(d_key)
    d_value[...] = jnp.zeros_like(d_value)
    for b in range(length // step):
        at = pl.ds(b * step, step)
        keys = (b + 1) * step
        allowed = allowed_pairs(begin[at, 0:1], b * step, step, keys)
        q = query[at, :]
        back = mm(g_all[at, :], w_out[...], NT).astype(bf16)
        product = back.astype(f32) * attended[at, :]
        result = jnp.zeros((step, cols), f32)
        for h in range(held):
            mine = head_lanes((step, cols), h)
            q_h = jnp.where(mine, q, jnp.zeros_like(q))
            back_h = jnp.where(mine, back, jnp.zeros_like(back))
            delta = jnp.sum(jnp.where(mine, product, 0.0), axis=1, keepdims=True)
            s = mm(q_h, key[:keys, :], NT) * scale
            p = jnp.exp(s - stats[at, 2 * h : 2 * h + 1]) * stats[at, 2 * h + 1 : 2 * h + 2]
            p = jnp.where(allowed, p, 0.0)
            d_p = mm(back_h, value[:keys, :], NT)
            d_s = (p * (d_p - delta)).astype(bf16)
            result = jnp.where(mine, mm(d_s, key[:keys, :]), result)
            d_key[:keys, :] += mm(d_s, q_h, TN)
            d_value[:keys, :] += mm(p.astype(bf16), back_h, TN)
        d_query[at, :] = result
    for b in range(length // step):
        at = pl.ds(b * step, step)
        c, s = cosine[at, :], sine[at, :]
        d_qkv[at, :cols] = turned(d_query[at, :] * scale, c, -s).astype(bf16)
        d_qkv[at, cols : 2 * cols] = turned(d_key[at, :] * scale, c, -s).astype(bf16)
        d_qkv[at, 2 * cols :] = d_value[at, :].astype(bf16)


def qkv_back(
    sizes, meta, g_all, weights, d_qkv, first_in, normed, vecs, part, sums, own24, pick24, own96, pick96,
    part_near, part_far, grads, place, base,
):
    f32, bf16 = jnp.float32, jnp.bfloat16
    nd, nc, per_d, held, nb, rows = sizes
    length, width = g_all.shape
    block = length // nc
    cols = held * HD
    ff = own96.shape[1]
    total = nd * nc
    w_qkv = weights[:, : 3 * cols]
    g_one = vecs[0:1, :]
    qkv_sum = jnp.zeros((1, 3 * cols), f32)
    gain_sum = jnp.zeros((1, width), f32)
    shift_sum = jnp.zeros((1, width), f32)
    for i in range(nc):
        half = part_near if i < nc // 2 else part_far
        at = pl.ds(pl.multiple_of(meta[i] * block, block), block)
        dq = d_qkv[at, :]
        qkv_sum += jnp.sum(dq.astype(f32), axis=0, keepdims=True)
        first = mm(dq, w_qkv, NT)
        gain_sum += jnp.sum(first * normed[at, :].astype(f32), axis=0, keepdims=True)
        shift_sum += jnp.sum(first, axis=0, keepdims=True)
        half[i % (nc // 2)] = (first * g_one + part[at, :].astype(f32)).astype(bf16)
    grad_qkv = mm(first_in[...], d_qkv[...], TN).astype(bf16)
    rows_d = width // nd
    for d in range(nd):
        grads[place(d), base : base + rows_d, :] = grad_qkv[d * rows_d : (d + 1) * rows_d]
    own = g_all[pl.ds(pl.multiple_of(meta[0] * block, block), block), :].astype(f32)
    own_sum = jnp.sum(own, axis=0, keepdims=True)

    def halves(row):
        high = row.astype(bf16).astype(f32)
        return high, row - high

    kept = iota((total, width), 0) == own24[...]
    up_owner = iota((total, ff), 0) == own96[...] * nc + meta[10]
    col_owner, col_place = column_places(meta, nb, cols, width, per_d, held)
    col_pick = (iota((block, 3 * cols), 0) == col_place).astype(f32).astype(bf16)
    col_kept = iota((total, 3 * cols), 0) == col_owner
    line = iota((total, 8, block), 1)
    packed = [jnp.zeros((total, 8, block), f32)] * 3
    entries = [
        (qkv_sum * meta[11].astype(f32), col_kept, col_pick),
        (sums[2:3, :ff], up_owner, pick96[...]),
        (own_sum, kept, pick24[...]),
        (gain_sum, kept, pick24[...]),
        (shift_sum, kept, pick24[...]),
        (sums[0:1, :], kept, pick24[...]),
        (sums[1:2, :], kept, pick24[...]),
    ]
    for k, (vector, where, pick) in enumerate(entries):
        for n, piece in enumerate(halves(vector)):
            spread = mm(jnp.where(where, piece, 0.0).astype(bf16), pick, NT)
            number = k + 8 * n
            packed[number % 3] = jnp.where(line == number // 3, spread[:, None, :], packed[number % 3])
    vector_rows = jnp.concatenate(packed, axis=2).reshape(nd, nc * 8, 3 * block).astype(bf16)
    for d in range(nd):
        grads[place(d), base + rows_d :, :] = vector_rows[d]


def backward_kernel(
    sizes, meta, near, far, weights, w_out, down, cosine, sine, begin, query, key, value, attended, stats, hidden, slope,
    first_in, second_in, normed, vecs, own24, pick24, own96, pick96,
    keep, give, part_near, part_far,
    g_all, part, sums, pre_grad, d_qkv, d_query, d_key, d_value, grads,
):
    nd, nc, rows = sizes[0], sizes[1], sizes[5]
    base = nc * rows + 2 * (down.shape[0] // nd) + 2 * HD

    def place(d):
        other = meta[12] ^ d
        return (other >> 1) + (other & 1) * 2

    mlp_back(
        sizes, meta, near, far, weights, down, attended, hidden, slope, second_in, normed, vecs, part, g_all, sums, pre_grad,
        grads, place,
    )
    attention_back(
        sizes, meta, g_all, w_out, cosine, sine, begin, query, key, value, attended, stats, d_qkv, d_query, d_key, d_value
    )
    qkv_back(
        sizes, meta, g_all, weights, d_qkv, first_in, normed, vecs, part, sums, own24, pick24, own96, pick96,
        part_near, part_far, grads, place, base,
    )
    keep[...] = grads[:2]
    give[...] = grads[2:]


def unpack_kernel(per_d, nd, units, rows, back, grad_qkv, grad_up, *vectors):
    f32 = jnp.float32
    nc = back.shape[0]
    held = nd // 2
    width = grad_qkv.shape[1] // 3
    cols = held * HD
    pieces = [None] * (3 * per_d * nd)
    ups = [None] * (nd * nc)
    total = jnp.zeros((8, 3 * 128), f32)
    for t in range(nc):
        group, half = HEAD_OF[t // 2], t % 2
        w = back[t].astype(f32)
        if group is not None:
            for part in range(3):
                for k in range(held):
                    at = part * cols + k * HD
                    pieces[part * per_d * nd + per_d * (held * half + k) + group] = w[rows : 2 * rows, at : at + HD]
        total = total + w[2 * rows :]
        for k in range(nd):
            ups[k * nc + t] = w[:rows, k * units : (k + 1) * units]
    grad_qkv[...] = jnp.concatenate(pieces, axis=1)
    grad_up[...] = jnp.concatenate(ups, axis=1)

    def kind(k):
        return total[k // 3 : k // 3 + 1, 128 * (k % 3) : 128 * (k % 3) + 128]

    for k, vector in enumerate(vectors):
        vector[...] = (kind(k) + kind(k + 8))[:, : vector.shape[1]]


def device_table(nd, nc):
    table = []
    for d in range(nd):
        for c in range(nc):
            group = HEAD_OF[c // 2]
            spare = c ^ 1 ^ (6 if c // 2 == 1 else 2)
            table.append([c ^ k for k in slot_order(nc)] + [c % 2, group or 0, c, int(group is not None), d, spare])
    return np.asarray(table, np.int32)


def final_kernel(inner, tokens, cotangent, m1, m2, m3, out):
    f32 = jnp.float32
    x = tokens[...].astype(f32)
    centered = x - jnp.mean(x, axis=1, keepdims=True)
    inverse = lax.rsqrt(jnp.mean(centered * centered, axis=1, keepdims=True) + eps)
    normed = centered * inverse
    n = inner[...] + m1[...].astype(f32) + m2[...].astype(f32) + m3[...].astype(f32)
    n = n - jnp.mean(n, axis=1, keepdims=True) - normed * jnp.mean(n * normed, axis=1, keepdims=True)
    out[...] = (cotangent[...].astype(f32) + n * inverse).astype(out.dtype)


def head_split_plan(
    tokens,
    segment_numbers,
    cotangent,
    query_key_value_weight,
    query_key_value_bias,
    output_matrix,
    output_bias,
    up_matrix,
    up_input_bias,
    down_matrix,
    down_output_bias,
    first_gain,
    first_shift,
    second_gain,
    second_shift,
):
    f32, bf16, i32 = jnp.float32, jnp.bfloat16, jnp.int32
    nd, nc = lax.axis_size("dp"), lax.axis_size("ctx")
    block, width = tokens.shape[1], tokens.shape[2]
    per_d = width // HD // nd
    held = nd // 2
    cols = held * HD
    rows = query_key_value_weight.shape[0]
    units = down_matrix.shape[0]
    ff = nd * units
    nb, nu = query_key_value_bias.shape[0], up_input_bias.shape[0]
    length = nc * block
    rows_d = nc * rows
    sizes = (nd, nc, per_d, held, nb, rows)
    d, c = lax.axis_index("dp"), lax.axis_index("ctx")
    pair_index, half = c // 2, c % 2
    group = jnp.where(pair_index == 3, 2, jnp.minimum(pair_index, 1))
    active = pair_index != 2
    lane = np.arange(width)
    own24 = jnp.asarray((lane // rows)[None], i32)
    pick24 = jnp.asarray(np.arange(block)[:, None] == lane[None] % rows, bf16)
    unit = np.arange(ff)
    own96 = jnp.asarray((unit // units)[None], i32)
    pick96 = jnp.asarray(np.arange(block)[:, None] == unit[None] % units, bf16)
    freq = jnp.asarray((10000.0 ** (-np.arange(ROT // 2) * 2.0 / ROT))[:, None], f32)

    vectors = [
        query_key_value_bias, up_input_bias, output_bias, down_output_bias, first_gain, first_shift, second_gain,
        second_shift, segment_numbers,
    ]
    lanes = 3 * cols + ff + block
    bits = list(range(2, nc, 2))
    target = active & ((d < nd // 2) == (half == 0))
    meta = jnp.asarray(device_table(nd, nc), i32)
    meta = lax.dynamic_index_in_dim(meta, d * nc + c, 0, False)
    payload = lambda count: like((count, rows, lanes), bf16)
    mine, to_two, to_four, to_six, _ = call(
        partial(message_kernel, per_d, nd, nc, units),
        [payload(3), payload(3), payload(2), payload(3), payload(nc)],
        [meta, query_key_value_weight, up_matrix, output_matrix] + [v.reshape(1, -1) for v in vectors],
        limit=VMEM_MOST,
    )
    two, four, six = swapped(to_two, 2), swapped(to_four, 4), swapped(to_six, 6)
    x_own = after(tokens[0], two)
    x_moved = [swapped(x_own, bit) for bit in bits]
    message_far = swapped(
        jnp.stack([mine[1], two[1], four[1], six[1], mine[2], jnp.where(pair_index == 1, six[2], two[2])]), 1
    )
    (package,) = call(
        package_kernel,
        [like((rows_d + units + HD, lanes), bf16)],
        [meta, mine, two, four, six, message_far, down_matrix],
        scratch=[pltpu.VMEM((nc, rows, lanes), f32)] * 2,
        limit=VMEM_MOST,
    )
    x_near = jnp.stack([after(tokens[0], package)] + x_moved)
    x_far = swapped(x_near, 1)
    g_own = after(cotangent[0], *x_moved)
    g_moved = [swapped(g_own, bit) for bit in bits]
    g_near = jnp.stack([g_own] + g_moved)
    g_far = swapped(after(g_near, x_far), 1)
    cosine, sine, begin = call(
        partial(tables_kernel, nc, rows), [like((length, cols), f32)] * 3, [package, freq], smem=False
    )
    across = swapped_dp(package, 2)
    own_pair = jnp.stack([package, after(across, cosine, x_far, *g_moved)])
    other_pair = swapped_dp(own_pair, 1)

    full = lambda dtype: like((length, width), dtype)
    part_shape = like((nc // 2, block, width), bf16)
    (
        out_near, out_far, first_in, second_in, normed, query, key, value, attended, stats, hidden, slope, vecs, weights,
        w_out, w_down,
    ) = call(
        partial(forward_kernel, sizes),
        [part_shape, part_shape, full(bf16), full(bf16), full(bf16)]
        + [like((length, cols), bf16)] * 3
        + [like((length, cols), f32), like((length, 128), f32)]
        + [like((length, ff), bf16)] * 2
        + [like((8, width), f32), like((width, 3 * cols + ff), bf16), like((cols, width), bf16), like((ff, width), bf16)],
        [meta, x_near, x_far, own_pair, other_pair, cosine, sine, begin, own24, pick24, own96, pick96],
        scratch=[pltpu.VMEM((nd, rows_d, lanes), bf16), pltpu.VMEM((nd, HD, width), bf16)],
        flops=FORWARD_WORK,
    )
    half_rows = rows_d + 2 * units + 2 * HD
    grad_rows = half_rows + rows_d + 8 * nc
    keep, give, n_near, n_far = call(
        partial(backward_kernel, sizes),
        [like((nd // 2, grad_rows, 3 * cols), bf16)] * 2 + [part_shape, part_shape],
        [meta, g_near, g_far, weights, w_out, w_down, cosine, sine, begin, query, key, value, attended, stats, hidden, slope,
         first_in, second_in, normed, vecs, own24, pick24, own96, pick96],
        scratch=[
            pltpu.VMEM((length, width), bf16),
            pltpu.VMEM((length, width), bf16),
            pltpu.VMEM((8, width), f32),
            pltpu.VMEM((length, ff), bf16),
            pltpu.VMEM((length, 3 * cols), bf16),
        ]
        + [pltpu.VMEM((length, cols), f32)] * 3
        + [pltpu.VMEM((nd, grad_rows, 3 * cols), bf16)],
        flops=BACKWARD_WORK,
    )

    def near_sum(near, far):
        total = near.astype(f32) + swapped(far, 1).astype(f32)
        return total, total.astype(bf16)

    out_total, out_low = near_sum(out_near, after(out_far, g_far))
    n_far, give = lax.optimization_barrier((n_far, give, out_low))[:2]
    grads = keep.astype(f32) + swapped_dp(give, 1).astype(f32)
    grads_low = grads[1].astype(bf16)
    out_low = after(out_low, grads_low)
    out_moved = [swapped(out_low[1 + k], bit) for k, bit in enumerate(bits)]
    grads_moved = swapped_dp(grads_low, 2)
    n_total, n_low = near_sum(after(n_near, out_moved[0]), n_far)
    n_low = after(n_low, out_moved[1], out_moved[2], grads_moved)
    n_moved = [swapped(n_low[1 + k], bit) for k, bit in enumerate(bits)]
    grads = grads[0] + after(grads_moved, n_moved[0]).astype(f32)
    mixed_sum = sum((m.astype(f32) for m in out_moved), out_total[0])
    mixed = (tokens[0].astype(f32) + (mixed_sum + vecs[4])).astype(bf16)
    (tokens_grad,) = call(
        final_kernel, [like((block, width), bf16)], [n_total[0], tokens[0], cotangent[0]] + n_moved, smem=False
    )
    at_out = rows_d + 2 * units
    at_qkv = at_out + 2 * HD
    at_vec = at_qkv + rows_d
    back = jnp.concatenate(
        [
            grads[:rows_d].reshape(nc, rows, ff),
            grads[at_qkv:at_vec].reshape(nc, rows, 3 * cols),
            grads[at_vec:].reshape(nc, 8, 3 * cols),
        ],
        axis=1,
    )
    back = lax.all_to_all(back.astype(bf16), "ctx", 0, 0, tiled=True)
    down_weight_grad = jnp.concatenate([grads[rows_d : rows_d + units], grads[rows_d + units : at_out]], axis=1)
    head_rows = jnp.concatenate([grads[at_out : at_out + HD], grads[at_out + HD : at_qkv]], axis=1).astype(bf16)
    head_rows = jnp.where(target, head_rows, jnp.zeros_like(head_rows))
    strip = lax.dynamic_update_slice(jnp.zeros((rows_d, width), bf16), head_rows, (HD * group, 0))
    strip = after(strip, n_moved[0], mixed)

    def strip_block(index):
        return lax.dynamic_slice_in_dim(strip, index * rows, rows, 0)

    third = jnp.where(group == 0, 2, jnp.where(group == 1, 4, 5))
    strips = [
        swapped(strip_block(c ^ 1), 1),
        sent(strip_block(third), lambda k: [(0, 2), (2, 4), (6, 5)] if k < nd // 2 else [(1, 2), (3, 4), (7, 5)]),
        sent(strip_block(jnp.int32(5)), lambda k: [(2, 5)] if k < nd // 2 else [(3, 5)]),
    ]
    out_weight_grad = sum((m.astype(f32) for m in strips), strip_block(c).astype(f32))

    qkv_weight_grad, up_weight_grad, *small = call(
        partial(unpack_kernel, per_d, nd, units, rows),
        [like((rows, 3 * width), f32), like((rows, nc * ff), f32), like((1, nb), f32), like((1, nu), f32)]
        + [like((1, rows), f32)] * 5,
        [back],
        smem=False,
    )
    small = [v.reshape(-1) for v in small]
    return (
        mixed[None],
        tokens_grad[None],
        qkv_weight_grad,
        small[0],
        out_weight_grad,
        small[2],
        up_weight_grad,
        small[1],
        down_weight_grad,
        small[2],
        small[3],
        small[4],
        small[5],
        small[6],
    )


def head_split_fits(nd, nc, width):
    return nd % 2 == 0 and width // HD == 3 * nd and nc == 8 and width // (nd * nc) * 8 == 3 * HD


def per_device(tokens, *others):
    nd, nc = lax.axis_size("dp"), lax.axis_size("ctx")
    plan = head_split_plan if head_split_fits(nd, nc, tokens.shape[2]) else gathered_plan
    return plan(tokens, *others)


def solution(mesh):
    in_specs = (
        P("dp", "ctx", None),
        P("dp", "ctx"),
        P("dp", "ctx", None),
        P(("dp", "ctx"), None),
        P(("dp", "ctx")),
        P(("dp", "ctx"), None),
        P(("dp", "ctx")),
        P(("dp", "ctx"), None),
        P(("dp", "ctx")),
        P(("dp", "ctx"), None),
        P(("dp", "ctx")),
        P(("dp", "ctx")),
        P(("dp", "ctx")),
        P(("dp", "ctx")),
        P(("dp", "ctx")),
    )
    out_specs = (
        P("dp", "ctx", None),
        P("dp", "ctx", None),
        P(("dp", "ctx"), None),
        P(("dp", "ctx")),
        P(("dp", "ctx"), None),
        P(("dp", "ctx")),
        P(("dp", "ctx"), None),
        P(("dp", "ctx")),
        P(("dp", "ctx"), None),
        P(("dp", "ctx")),
        P(("dp", "ctx")),
        P(("dp", "ctx")),
        P(("dp", "ctx")),
        P(("dp", "ctx")),
    )
    return jax.shard_map(
        per_device, mesh=mesh, in_specs=in_specs, out_specs=out_specs, check_vma=False
    )
```

```python
from functools import partial
import math

import jax
import jax.numpy as jnp
import numpy as np
from jax import lax
from jax.experimental import pallas as pl
from jax.experimental.pallas import tpu as pltpu
from jax.sharding import PartitionSpec as P

HD = 64
ROT = 16


eps = 1e-05


def rotation_tables(position):
    half = ROT // 2
    freq = 10000.0 ** (-jnp.arange(half, dtype=jnp.float32) * 2.0 / ROT)
    angle = position.astype(jnp.float32)[..., None] * freq
    return (jnp.cos(angle)[..., None, :], jnp.sin(angle)[..., None, :])


def rotate(field, cosine, sine):
    half = ROT // 2
    first = field[..., :half]
    second = field[..., half:ROT]
    return jnp.concatenate(
        [first * cosine - second * sine, second * cosine + first * sine, field[..., ROT:]], axis=-1
    )


def rotate_back(grad, cosine, sine):
    half = ROT // 2
    first = grad[..., :half]
    second = grad[..., half:ROT]
    return jnp.concatenate(
        [first * cosine + second * sine, second * cosine - first * sine, grad[..., ROT:]], axis=-1
    )


def over_blocks(step, carry, piece, start_offset):
    width = piece[0].shape[1]
    block_length = math.gcd(width, 512)
    token_count = width // block_length

    def advance(number, state):
        offset = number * block_length
        part = tuple((lax.dynamic_slice_in_dim(p, offset, block_length, 1) for p in piece))
        return step(state, part, start_offset + offset)

    return lax.fori_loop(0, token_count, advance, carry)


def scores_masked(query_rows, key, query_index, query_segment, key_index, key_segment):
    seqs, width = (key.shape[0], key.shape[1])
    keys = key.reshape(seqs, width, query_rows.shape[2], HD)
    score_matrix = jnp.einsum(
        "sqhd,skhd->shqk", query_rows, keys, preferred_element_type=jnp.float32
    ) * HD ** (-0.5)
    allowed_pairs = (key_index[None, None, :] <= query_index[None, :, None]) & (
        key_segment[:, None, :] == query_segment[:, :, None]
    )
    return (score_matrix, allowed_pairs[:, None])


def gathered_plan(
    tokens,
    segment_numbers,
    cotangent,
    query_key_value_weight,
    query_key_value_bias,
    output_matrix,
    output_bias,
    up_matrix,
    up_input_bias,
    down_matrix,
    down_output_bias,
    first_gain,
    first_shift,
    second_gain,
    second_shift,
):
    seqs, block, width = tokens.shape
    heads = width // HD
    rows = seqs * block
    scale = HD ** (-0.5)
    w_qkv, b_qkv, w_out, b_out, w_up, b_up, w_down, b_down, g_one, s_one, g_two, s_two = (
        lax.all_gather(query_key_value_weight, ("dp", "ctx"), axis=0, tiled=True),
        lax.all_gather(query_key_value_bias, ("dp", "ctx"), axis=0, tiled=True),
        lax.all_gather(output_matrix, ("dp", "ctx"), axis=0, tiled=True),
        lax.all_gather(output_bias, ("dp", "ctx"), axis=0, tiled=True),
        lax.all_gather(up_matrix, ("dp", "ctx"), axis=0, tiled=True),
        lax.all_gather(up_input_bias, ("dp", "ctx"), axis=0, tiled=True),
        lax.all_gather(down_matrix, ("dp", "ctx"), axis=0, tiled=True),
        lax.all_gather(down_output_bias, ("dp", "ctx"), axis=0, tiled=True),
        lax.all_gather(first_gain, ("dp", "ctx"), axis=0, tiled=True),
        lax.all_gather(first_shift, ("dp", "ctx"), axis=0, tiled=True),
        lax.all_gather(second_gain, ("dp", "ctx"), axis=0, tiled=True),
        lax.all_gather(second_shift, ("dp", "ctx"), axis=0, tiled=True),
    )
    seg_all = lax.all_gather(segment_numbers, "ctx", axis=1, tiled=True)
    length = seg_all.shape[1]
    index_all = jnp.arange(length, dtype=jnp.int32)
    fresh = jnp.concatenate(
        [jnp.ones((seqs, 1), jnp.bool_), seg_all[:, 1:] != seg_all[:, :-1]], axis=1
    )
    starts = lax.cummax(jnp.where(fresh, index_all[None, :], jnp.zeros_like(seg_all)), axis=1)
    offset = lax.axis_index("ctx") * block
    query_index = offset + jnp.arange(block, dtype=jnp.int32)
    position = query_index[None, :] - lax.dynamic_slice_in_dim(starts, offset, block, 1)
    cosine, sine = rotation_tables(position)
    xval = tokens.reshape(rows, width).astype(jnp.float32)
    mean = jnp.mean(xval, axis=-1, keepdims=True)
    centered = xval - mean
    inverse = lax.rsqrt(jnp.mean(centered * centered, axis=-1, keepdims=True) + eps)
    normed = centered * inverse
    first_input = (normed * g_one.astype(jnp.float32) + s_one.astype(jnp.float32)).astype(
        jnp.bfloat16
    )
    second_input = (normed * g_two.astype(jnp.float32) + s_two.astype(jnp.float32)).astype(
        jnp.bfloat16
    )
    query_key_value = jnp.dot(
        first_input, w_qkv, preferred_element_type=jnp.float32
    ) + b_qkv.astype(jnp.float32)
    query_key_value = query_key_value.reshape(seqs, block, 3 * width)
    query_block = rotate(
        query_key_value[..., :width].reshape(seqs, block, heads, HD), cosine, sine
    ).astype(jnp.bfloat16)
    key_b = (
        rotate(
            query_key_value[..., width : 2 * width].reshape(seqs, block, heads, HD), cosine, sine
        )
        .astype(jnp.bfloat16)
        .reshape(seqs, block, width)
    )
    value_b = query_key_value[..., 2 * width :].astype(jnp.bfloat16)

    def forward_step(carry, piece, start_offset):
        top, total, acc = carry
        key, value_rows = piece
        token_count = key.shape[1]
        key_index = start_offset + jnp.arange(token_count, dtype=jnp.int32)
        key_segment = lax.dynamic_slice_in_dim(seg_all, start_offset, token_count, 1)
        score_matrix, allowed_pairs = scores_masked(
            query_block, key, query_index, segment_numbers, key_index, key_segment
        )
        masked = jnp.where(allowed_pairs, score_matrix, -1e30)
        new_top = jnp.maximum(top, jnp.max(masked, axis=-1))
        weights = jnp.where(allowed_pairs, jnp.exp(masked - new_top[..., None]), 0.0)
        decay = jnp.exp(top - new_top)
        values = value_rows.reshape(seqs, token_count, heads, HD)
        total = total * decay + jnp.sum(weights, axis=-1)
        acc = acc * decay[..., None] + jnp.einsum(
            "shqk,skhd->shqd",
            weights.astype(jnp.bfloat16),
            values,
            preferred_element_type=jnp.float32,
        )
        return (new_top, total, acc)

    init = (
        jnp.full((seqs, heads, block), -1e30, jnp.float32),
        jnp.zeros((seqs, heads, block), jnp.float32),
        jnp.zeros((seqs, heads, block, HD), jnp.float32),
    )
    top, total, acc = over_blocks(
        forward_step,
        init,
        (
            lax.all_gather(key_b, "ctx", axis=1, tiled=True),
            lax.all_gather(value_b, "ctx", axis=1, tiled=True),
        ),
        jnp.int32(0),
    )
    attended_output = acc / total[..., None]
    log_sum_exp = top + jnp.log(total)
    attended_rows = attended_output.transpose(0, 2, 1, 3).reshape(rows, width)
    attended_b = attended_rows.astype(jnp.bfloat16)
    attention_block = jnp.dot(attended_b, w_out, preferred_element_type=jnp.float32) + b_out.astype(
        jnp.float32
    )
    pre_activation = jnp.dot(second_input, w_up, preferred_element_type=jnp.float32) + b_up.astype(
        jnp.float32
    )
    hidden_state, gelu_back = jax.vjp(partial(jax.nn.gelu, approximate=False), pre_activation)
    hidden_b = hidden_state.astype(jnp.bfloat16)
    feed_forward = jnp.dot(hidden_b, w_down, preferred_element_type=jnp.float32) + b_down.astype(
        jnp.float32
    )
    mixed = (xval + attention_block + feed_forward).astype(jnp.bfloat16).reshape(seqs, block, width)
    v_qkv, v_out, v_up, v_down, h_one, h_two = (
        lax.all_gather(query_key_value_weight, ("dp", "ctx"), axis=0, tiled=True),
        lax.all_gather(output_matrix, ("dp", "ctx"), axis=0, tiled=True),
        lax.all_gather(up_matrix, ("dp", "ctx"), axis=0, tiled=True),
        lax.all_gather(down_matrix, ("dp", "ctx"), axis=0, tiled=True),
        lax.all_gather(first_gain, ("dp", "ctx"), axis=0, tiled=True),
        lax.all_gather(second_gain, ("dp", "ctx"), axis=0, tiled=True),
    )
    kv_all = (
        lax.all_gather(key_b, "ctx", axis=1, tiled=True),
        lax.all_gather(value_b, "ctx", axis=1, tiled=True),
    )
    cot_b = cotangent.reshape(rows, width)
    cot = cot_b.astype(jnp.float32)
    grad_down_w = jnp.dot(hidden_b.T, cot_b, preferred_element_type=jnp.float32)
    grad_down_b = jnp.sum(cot, axis=0)
    grad_out_w = jnp.dot(attended_b.T, cot_b, preferred_element_type=jnp.float32)
    hidden_grad = jnp.dot(cot_b, v_down.T, preferred_element_type=jnp.float32)
    pre_grad = gelu_back(hidden_grad)[0].astype(jnp.bfloat16)
    grad_up_w = jnp.dot(second_input.T, pre_grad, preferred_element_type=jnp.float32)
    grad_up_b = jnp.sum(pre_grad.astype(jnp.float32), axis=0)
    second_grad = jnp.dot(pre_grad, v_up.T, preferred_element_type=jnp.float32)
    attended_grad = jnp.dot(cot_b, v_out.T, preferred_element_type=jnp.float32).astype(jnp.bfloat16)
    output_gradient_block = attended_grad.reshape(seqs, block, heads, HD)
    outgrad_f = output_gradient_block.astype(jnp.float32)
    delta_terms = jnp.sum(outgrad_f.transpose(0, 2, 1, 3) * attended_output, axis=-1)

    def pair_gradients(
        query_portion,
        gradient_portion,
        logsum_portion,
        delta_portion,
        query_position,
        query_segment,
        key,
        value_rows,
        key_index,
        key_segment,
    ):
        token_count = key.shape[1]
        score_matrix, allowed_pairs = scores_masked(
            query_portion, key, query_position, query_segment, key_index, key_segment
        )
        weights = jnp.where(allowed_pairs, jnp.exp(score_matrix - logsum_portion[..., None]), 0.0)
        values = value_rows.reshape(seqs, token_count, heads, HD)
        prob_grad = jnp.einsum(
            "sqhd,skhd->shqk", gradient_portion, values, preferred_element_type=jnp.float32
        )
        score_grad = (weights * (prob_grad - delta_portion[..., None])).astype(jnp.bfloat16)
        return (weights, score_grad)

    def query_step(carry, piece, start_offset):
        key, value_rows = piece
        token_count = key.shape[1]
        key_index = start_offset + jnp.arange(token_count, dtype=jnp.int32)
        key_segment = lax.dynamic_slice_in_dim(seg_all, start_offset, token_count, 1)
        weights, score_grad = pair_gradients(
            query_block,
            output_gradient_block,
            log_sum_exp,
            delta_terms,
            query_index,
            segment_numbers,
            key,
            value_rows,
            key_index,
            key_segment,
        )
        keys = key.reshape(seqs, token_count, heads, HD)
        return (
            carry
            + jnp.einsum("shqk,skhd->shqd", score_grad, keys, preferred_element_type=jnp.float32)
            * scale
        )

    query_grad = over_blocks(
        query_step, jnp.zeros((seqs, heads, block, HD), jnp.float32), kv_all, 0
    )
    token_count = block * lax.axis_size("ctx")
    block_length = math.gcd(token_count, 512)

    def one_block(number):
        begin_offset = number * block_length
        key = lax.dynamic_slice_in_dim(kv_all[0], begin_offset, block_length, 1)
        value_rows = lax.dynamic_slice_in_dim(kv_all[1], begin_offset, block_length, 1)
        key_index = begin_offset + jnp.arange(block_length, dtype=jnp.int32)
        key_segment = lax.dynamic_slice_in_dim(seg_all, begin_offset, block_length, 1)
        weights, score_grad = pair_gradients(
            query_block,
            output_gradient_block,
            log_sum_exp,
            delta_terms,
            query_index,
            segment_numbers,
            key,
            value_rows,
            key_index,
            key_segment,
        )
        key_grad = (
            jnp.einsum(
                "shqk,sqhd->skhd", score_grad, query_block, preferred_element_type=jnp.float32
            )
            * scale
        )
        value_grad = jnp.einsum(
            "shqk,sqhd->skhd",
            weights.astype(jnp.bfloat16),
            output_gradient_block,
            preferred_element_type=jnp.float32,
        )
        paired = jnp.concatenate(
            [
                key_grad.reshape(seqs, block_length, width),
                value_grad.reshape(seqs, block_length, width),
            ],
            axis=-1,
        )
        return paired.transpose(1, 0, 2)

    parts = lax.map(one_block, jnp.arange(token_count // block_length, dtype=jnp.int32))
    kv_grad = lax.psum_scatter(
        parts.reshape(token_count, seqs, 2 * width), "ctx", scatter_dimension=0, tiled=True
    ).transpose(1, 0, 2)
    query_back = rotate_back(query_grad.transpose(0, 2, 1, 3), cosine, sine).reshape(
        seqs, block, width
    )
    key_back = rotate_back(
        kv_grad[..., :width].reshape(seqs, block, heads, HD), cosine, sine
    ).reshape(seqs, block, width)
    qkv_grad = (
        jnp.concatenate([query_back, key_back, kv_grad[..., width:]], axis=-1)
        .reshape(rows, 3 * width)
        .astype(jnp.bfloat16)
    )
    grad_qkv_w = jnp.dot(first_input.T, qkv_grad, preferred_element_type=jnp.float32)
    grad_qkv_b = jnp.sum(qkv_grad.astype(jnp.float32), axis=0)
    first_grad = jnp.dot(qkv_grad, v_qkv.T, preferred_element_type=jnp.float32)
    grad_g_one = jnp.sum(normed * first_grad, axis=0)
    grad_s_one = jnp.sum(first_grad, axis=0)
    grad_g_two = jnp.sum(normed * second_grad, axis=0)
    grad_s_two = jnp.sum(second_grad, axis=0)
    normed_grad = first_grad * h_one.astype(jnp.float32) + second_grad * h_two.astype(jnp.float32)
    inner = (
        normed_grad
        - jnp.mean(normed_grad, axis=-1, keepdims=True)
        - normed * jnp.mean(normed_grad * normed, axis=-1, keepdims=True)
    )
    tokens_grad = (cot + inner * inverse).astype(jnp.bfloat16).reshape(seqs, block, width)
    shards = (
        lax.psum_scatter(grad_qkv_w, ("dp", "ctx"), scatter_dimension=0, tiled=True),
        lax.psum_scatter(grad_qkv_b, ("dp", "ctx"), scatter_dimension=0, tiled=True),
        lax.psum_scatter(grad_out_w, ("dp", "ctx"), scatter_dimension=0, tiled=True),
        lax.psum_scatter(grad_down_b, ("dp", "ctx"), scatter_dimension=0, tiled=True),
        lax.psum_scatter(grad_up_w, ("dp", "ctx"), scatter_dimension=0, tiled=True),
        lax.psum_scatter(grad_up_b, ("dp", "ctx"), scatter_dimension=0, tiled=True),
        lax.psum_scatter(grad_down_w, ("dp", "ctx"), scatter_dimension=0, tiled=True),
        lax.psum_scatter(grad_down_b, ("dp", "ctx"), scatter_dimension=0, tiled=True),
        lax.psum_scatter(grad_g_one, ("dp", "ctx"), scatter_dimension=0, tiled=True),
        lax.psum_scatter(grad_s_one, ("dp", "ctx"), scatter_dimension=0, tiled=True),
        lax.psum_scatter(grad_g_two, ("dp", "ctx"), scatter_dimension=0, tiled=True),
        lax.psum_scatter(grad_s_two, ("dp", "ctx"), scatter_dimension=0, tiled=True),
    )
    return (mixed, tokens_grad) + tuple(shards)


VMEM_LIMIT = 30 * 1024 * 1024
VMEM_MOST = 56 * 1024 * 1024
FORWARD_WORK = 10**8
BACKWARD_WORK = 10**8
NT = (((1,), (1,)), ((), ()))
TN = (((0,), (0,)), ((), ()))
NN = (((1,), (0,)), ((), ()))


def mm(a, b, dims=NN):
    return lax.dot_general(a, b, dims, preferred_element_type=jnp.float32)


HEAD_OF = (0, 1, None, 2)


def vmem(count):
    return [pl.BlockSpec(memory_space=pltpu.VMEM)] * count


def call(kernel, outs, operands, scratch=(), flops=0, smem=True, limit=VMEM_LIMIT):
    specs = vmem(len(operands))
    if smem:
        specs[0] = pl.BlockSpec(memory_space=pltpu.SMEM)
    return pl.pallas_call(
        kernel,
        out_shape=[jax.ShapeDtypeStruct(o.shape, o.dtype) for o in outs],
        in_specs=specs,
        out_specs=vmem(len(outs)),
        scratch_shapes=list(scratch),
        compiler_params=pltpu.CompilerParams(vmem_limit_bytes=limit),
        cost_estimate=pl.CostEstimate(flops=flops, bytes_accessed=1024, transcendentals=0),
    )(*operands)


def like(shape, dtype):
    return jax.ShapeDtypeStruct(shape, dtype)


def slot_order(size):
    return list(range(0, size, 2)) + list(range(1, size, 2))


def swapped(x, bit):
    size = lax.axis_size("ctx")
    return lax.ppermute(x, "ctx", [(i, i ^ bit) for i in range(size)])


def swapped_dp(x, bit):
    size = lax.axis_size("dp")
    return lax.ppermute(x, "dp", [(i, i ^ bit) for i in range(size)])


def after(x, *others):
    return lax.optimization_barrier((x,) + others)[0]


def sent(x, pairs):
    nd, nc = lax.axis_size("dp"), lax.axis_size("ctx")
    flat = [(d * nc + a, d * nc + b) for d in range(nd) for a, b in pairs(d)]
    return lax.ppermute(x, ("dp", "ctx"), flat)


def gathered_block(meta, i, pairs):
    return 2 * (i % pairs) + ((meta[8] + i // pairs) & 1)


def pair_exchange(x):
    size = lax.axis_size("ctx")
    groups = [list(range(half, size, 2)) for half in range(2)]
    return lax.all_to_all(x, "ctx", 0, 0, axis_index_groups=groups, tiled=True)


def iota(shape, dim):
    return lax.broadcasted_iota(jnp.int32, shape, dim)


def message_kernel(per_d, nd, nc, units, meta, qkv, up, out_rows, *refs):
    f32 = jnp.float32
    vectors, out = refs[:-5], refs[-1]
    mine, two, four, six = refs[-5:-1]
    c = meta[10]
    rows = qkv.shape[0]
    width = qkv.shape[1] // 3
    held = nd // 2
    w = qkv[...].astype(f32)
    u = up[...].astype(f32)
    lines = []
    for vector in vectors:
        line = vector[...].astype(f32)
        if line.shape[1] < 128:
            line = jnp.concatenate([line, jnp.zeros((1, 128 - line.shape[1]), f32)], axis=1)
        lines.append(line)
    v = jnp.concatenate(lines + [jnp.zeros((rows - len(lines), 128), f32)], axis=0)
    for t in range(nc):
        group, half = HEAD_OF[t // 2], t % 2
        pieces = []
        for part in range(3):
            for k in range(held):
                at = part * width + HD * (per_d * (held * half + k) + (group or 0))
                pieces.append(jnp.zeros((rows, HD), f32) if group is None else w[:, at : at + HD])
        for k in range(nd):
            at = k * nc * units + t * units
            pieces.append(u[:, at : at + units])
        out[c ^ t] = jnp.concatenate(pieces + [v], axis=1).astype(out.dtype)
    blank = jnp.zeros((rows, out.shape[2] - width), f32)
    head = jnp.concatenate([out_rows[...].astype(f32), blank], axis=1).astype(out.dtype)
    mine[0], mine[1], mine[2] = out[0], out[1], head
    two[0], two[1], two[2] = out[2], out[3], head
    four[0], four[1] = out[4], out[5]
    six[0], six[1], six[2] = out[6], out[7], head


def package_kernel(meta, mine, two, four, six, far, down, out, natural, strip):
    f32 = jnp.float32
    nc, rows, lanes = natural.shape
    c = meta[10]
    width = down.shape[1]
    for k, near in enumerate((mine, two, four, six)):
        natural[c ^ (2 * k)] = near[0].astype(f32)
        natural[c ^ (2 * k + 1)] = far[k].astype(f32)
    out[: nc * rows, :] = natural[...].reshape(nc * rows, lanes).astype(out.dtype)
    strip[...] = jnp.zeros_like(strip)
    strip[c] = mine[2].astype(f32)
    strip[c ^ 2] = two[2].astype(f32)
    strip[c ^ 6] = six[2].astype(f32)
    strip[c ^ 1] = far[4].astype(f32)
    strip[meta[13]] = far[5].astype(f32)
    whole = strip[...].reshape(nc * rows, lanes)
    group = meta[9]
    head = jnp.where(group == 0, whole[:HD], jnp.where(group == 1, whole[HD : 2 * HD], whole[2 * HD : 3 * HD]))
    tail = jnp.concatenate([down[...].astype(f32), head[:, :width]], axis=0)
    blank = jnp.zeros((tail.shape[0], lanes - width), f32)
    out[nc * rows :, :] = jnp.concatenate([tail, blank], axis=1).astype(out.dtype)


def tables_kernel(nc, rows, package, freq, cosine, sine, begin):
    f32 = jnp.float32
    lanes = package.shape[1]
    block = 128
    head = package[: nc * rows, lanes - block :].astype(f32).reshape(nc, rows, block)
    seg = jnp.sum(jnp.where(iota((nc, rows, block), 1) == 8, head, 0.0), axis=1)
    start = jnp.zeros((nc, block), f32)
    for number in range(1, 8):
        earlier = jnp.where(seg < number, 1.0, 0.0)
        count = jnp.sum(jnp.sum(earlier, axis=1, keepdims=True), axis=0, keepdims=True)
        start = jnp.where(seg == number, count, start)
    index = (iota((nc, block), 0) * block + iota((nc, block), 1)).astype(f32)

    def as_row(x):
        return jnp.concatenate([x[b : b + 1] for b in range(nc)], axis=1)

    half = ROT // 2
    angle = freq[...] * as_row(index - start)
    table = jnp.concatenate(
        [jnp.cos(angle), jnp.sin(angle), jnp.broadcast_to(as_row(start), angle.shape)], axis=0
    )
    feature = iota((3 * half, block), 1) % HD
    row = iota((3 * half, block), 0)
    first, second = feature == row, feature == row + half
    rotary = feature < ROT
    is_first, is_second = jnp.where(first & rotary, 1.0, 0.0), jnp.where(second & rotary, 1.0, 0.0)
    pick_cos = jnp.where(row < half, is_first + is_second, 0.0)
    row2 = row - half
    sine_first = jnp.where((feature == row2) & rotary & (row2 >= 0), -1.0, 0.0)
    sine_second = jnp.where((feature == row2 + half) & rotary & (row2 >= 0), 1.0, 0.0)
    pick_sin = jnp.where(row < 2 * half, sine_first + sine_second, 0.0)
    pick_start = jnp.where(row == 2 * half, 1.0, 0.0)

    def spread(pick):
        return lax.dot_general(
            table, pick, TN, precision=lax.Precision.HIGHEST, preferred_element_type=f32
        )

    still = jnp.where(iota((1, block), 1) % HD < ROT, 0.0, 1.0)
    cosine[...] = spread(pick_cos) + still
    sine[...] = spread(pick_sin)
    begin[...] = spread(pick_start)


def turned(t, cosine, sine):
    lanes = t.shape[1]
    early = iota(t.shape, 1) % HD < ROT // 2
    other = jnp.where(early, pltpu.roll(t, lanes - ROT // 2, 1), pltpu.roll(t, ROT // 2, 1))
    return t * cosine + other * sine


def allowed_pairs(begin, first_row, rows, keys):
    key_index = iota((rows, keys), 1)
    query_index = iota((rows, keys), 0) + first_row
    return (key_index <= query_index) & (key_index >= begin.astype(jnp.int32))


def head_lanes(shape, h):
    lane = iota(shape, 1)
    return (lane >= h * HD) & (lane < (h + 1) * HD)


def column_places(meta, nb, cols, width, per_d, held):
    j = iota((1, 3 * cols), 1)
    part = jnp.where(j >= 2 * cols, 2, jnp.where(j >= cols, 1, 0))
    rest = j - part * cols
    hh = jnp.zeros_like(rest)
    for k in range(1, held):
        hh = hh + jnp.where(rest >= k * HD, 1, 0)
    column = part * width + hh * (per_d * HD) + (rest - hh * HD)
    column = column + HD * (per_d * held * meta[8] + meta[9])
    owner = jnp.floor((column.astype(jnp.float32) + 0.5) / nb).astype(jnp.int32)
    return owner, column - owner * nb


def forward_kernel(
    sizes, meta, near, far, own_pair, other_pair, cosine, sine, begin, own24, pick24, own96, pick96,
    out_near, out_near_own, out_far, out_far_own, first_in, second_in, normed, query, key, value, attended, probs, hidden, slope, vecs, weights,
    w_out, down, every, outs,
):
    f32, bf16 = jnp.float32, jnp.bfloat16
    nd, nc, per_d, held, nb, rows = sizes
    block, width = near.shape[1], near.shape[2]
    cols = held * HD
    ff = own96.shape[1]
    length = nc * block
    total = nd * nc
    n1 = nc * rows
    n2 = n1 + ff // nd
    for i, pair in enumerate((own_pair, other_pair) * 2):
        other = meta[12] ^ i
        piece = pair.at[i // 2]
        every[other] = piece[:n1]
        down[pl.ds(pl.multiple_of(other * (ff // nd), ff // nd), ff // nd), :] = piece[n1:n2, :width]
        outs[other] = piece[n2:, :width]
    w_out[...] = outs[pl.ds(held * meta[8], held)].reshape(cols, width)
    weights[...] = every[:, :, : 3 * cols + ff].reshape(width, 3 * cols + ff)
    packed = every[:, :, 3 * cols + ff :].astype(f32).reshape(total, rows, block)
    kind = iota(packed.shape, 1)

    def of_kind(k):
        return jnp.sum(jnp.where(kind == k, packed, 0.0), axis=1).astype(bf16)

    owner = iota((total, width), 0)
    kept = owner == own24[...]
    flat = []
    for k in range(2, 8):
        flat.append(jnp.sum(jnp.where(kept, mm(of_kind(k), pick24[...]), 0.0), axis=0, keepdims=True))
    out_bias, g_one, s_one, g_two, s_two = flat[0] + flat[1], flat[2], flat[3], flat[4], flat[5]
    up_owner = iota((total, ff), 0) == own96[...] * nc + meta[10]
    b_up = jnp.sum(jnp.where(up_owner, mm(of_kind(1), pick96[...]), 0.0), axis=0, keepdims=True)
    col_owner, col_place = column_places(meta, nb, cols, width, per_d, held)
    col_pick = (iota((block, 3 * cols), 0) == col_place).astype(f32).astype(bf16)
    b_qkv = jnp.where(iota((total, 3 * cols), 0) == col_owner, mm(of_kind(0), col_pick), 0.0)
    b_qkv = jnp.sum(b_qkv, axis=0, keepdims=True) * meta[11].astype(f32)
    for k, vector in enumerate((g_one, s_one, g_two, s_two, out_bias)):
        vecs[k : k + 1, :] = vector
    for i in range(nc):
        half = near if i < nc // 2 else far
        x = half[i % (nc // 2)].astype(f32)
        centered = x - jnp.mean(x, axis=1, keepdims=True)
        n = centered * lax.rsqrt(jnp.mean(centered * centered, axis=1, keepdims=True) + eps)
        at = pl.ds(pl.multiple_of(gathered_block(meta, i, nc // 2) * block, block), block)
        normed[at, :] = n.astype(bf16)
        first_in[at, :] = (n * g_one + s_one).astype(bf16)
        second_in[at, :] = (n * g_two + s_two).astype(bf16)
    w_qkv = weights[:, : 3 * cols]
    w_up = weights[:, 3 * cols :]
    step = 2 * block
    for b in range(length // step):
        at = pl.ds(b * step, step)
        t = mm(first_in[at, :], w_qkv) + b_qkv
        query[at, :] = (turned(t[:, :cols], cosine[at, :], sine[at, :])).astype(bf16)
        key[at, :] = turned(t[:, cols : 2 * cols], cosine[at, :], sine[at, :]).astype(bf16)
        value[at, :] = t[:, 2 * cols :].astype(bf16)
    for b in range(length // step):
        at = pl.ds(b * step, step)
        pre = mm(second_in[at, :], w_up) + b_up
        cdf = 0.5 + 0.5 * lax.erf(pre * (0.5**0.5))
        hidden[at, :] = (pre * cdf).astype(bf16)
        slope[at, :] = (cdf + pre * jnp.exp(-0.5 * pre * pre) * ((2 * math.pi) ** -0.5)).astype(bf16)
    for b in range(length // step):
        at = pl.ds(b * step, step)
        keys = (b + 1) * step
        allowed = allowed_pairs(begin[at, 0:1], b * step, step, keys)
        q = query[at, :]
        result = jnp.zeros((step, cols), f32)
        for h in range(held):
            mine = head_lanes((step, cols), h)
            s = mm(jnp.where(mine, q, jnp.zeros_like(q)), key[:keys, :], NT) * (HD**-0.5)
            s = jnp.where(allowed, s, -1e30)
            top = jnp.max(s, axis=1, keepdims=True)
            p = jnp.exp(s - top)
            inverse = 1.0 / jnp.sum(p, axis=1, keepdims=True)
            low = (p * inverse).astype(bf16)
            probs[h, at, :keys] = low
            result = jnp.where(mine, mm(low, value[:keys, :]), result)
        attended[at, :] = result
    for i in range(nc):
        slot = i % (nc // 2)
        rest, own = (out_near, out_near_own) if i < nc // 2 else (out_far, out_far_own)
        at = pl.ds(pl.multiple_of(meta[i] * block, block), block)
        piece = mm(attended[at, :].astype(bf16), w_out[...]) + mm(hidden[at, :], down[...])
        if slot == 0:
            own[...] = piece.astype(bf16)
        else:
            rest[slot - 1] = piece.astype(bf16)


def mlp_back(
    sizes, meta, near, far, weights, down, attended, hidden, slope, second_in, normed, vecs, part, g_all, sums, pre_grad,
    grads, place,
):
    f32, bf16 = jnp.float32, jnp.bfloat16
    nd, nc, per_d, held, nb, rows = sizes
    block, width = near.shape[1], near.shape[2]
    cols = held * HD
    ff = down.shape[0]
    units = ff // nd
    length = nc * block
    for i in range(nc):
        half = near if i < nc // 2 else far
        at = pl.ds(pl.multiple_of(meta[i] * block, block), block)
        g_all[at, :] = half[i % (nc // 2)]
    g = g_all[...]
    rows_d = width // nd
    side = width // 2

    grad_down = mm(hidden[...], g, TN).astype(bf16)
    for d in range(nd):
        piece = grad_down[d * units : (d + 1) * units]
        slot = place(d)
        grads[slot, rows_d : rows_d + units, :] = piece[:, :side]
        grads[slot, rows_d + units : rows_d + 2 * units, :] = piece[:, side:]
    grad_out = mm(attended[...].astype(bf16), g, TN)
    base = rows_d + 2 * units
    for d in range(nd):
        here = (meta[8] == d // held) & (meta[11] == 1)
        k = d % held
        piece = jnp.where(here, grad_out[k * HD : (k + 1) * HD], 0.0).astype(bf16)
        slot = place(d)
        grads[slot, base : base + HD, :] = piece[:, :side]
        grads[slot, base + HD : base + 2 * HD, :] = piece[:, side:]
    step = 2 * block
    w_up = weights[:, 3 * cols :]
    g_two = vecs[2:3, :]
    up_sum = jnp.zeros((1, ff), f32)
    gain_sum = jnp.zeros((1, width), f32)
    shift_sum = jnp.zeros((1, width), f32)
    for b in range(length // step):
        at = pl.ds(b * step, step)
        back = (mm(g_all[at, :], down[...], NT) * slope[at, :].astype(f32)).astype(bf16)
        pre_grad[at, :] = back
        up_sum += jnp.sum(back.astype(f32), axis=0, keepdims=True)
        second = mm(back, w_up, NT)
        gain_sum += jnp.sum(second * normed[at, :].astype(f32), axis=0, keepdims=True)
        shift_sum += jnp.sum(second, axis=0, keepdims=True)
        part[at, :] = (second * g_two).astype(bf16)
    sums[0:1, :] = gain_sum
    sums[1:2, :] = shift_sum
    sums[2:3, :ff] = up_sum
    grad_up = mm(second_in[...], pre_grad[...], TN).astype(bf16)
    for d in range(nd):
        grads[place(d), :rows_d, :] = grad_up[d * rows_d : (d + 1) * rows_d]


def attention_back(
    sizes, meta, g_all, w_out, cosine, sine, query, key, value, attended, probs, d_qkv, d_query, d_key, d_value
):
    f32, bf16 = jnp.float32, jnp.bfloat16
    nd, nc, per_d, held, nb, rows = sizes
    length, width = g_all.shape
    block = length // nc
    cols = held * HD
    step = 2 * block
    scale = HD**-0.5
    d_key[...] = jnp.zeros_like(d_key)
    d_value[...] = jnp.zeros_like(d_value)
    for b in range(length // step):
        at = pl.ds(b * step, step)
        keys = (b + 1) * step
        q = query[at, :]
        back = mm(g_all[at, :], w_out[...], NT).astype(bf16)
        product = back.astype(f32) * attended[at, :]
        result = jnp.zeros((step, cols), f32)
        for h in range(held):
            mine = head_lanes((step, cols), h)
            q_h = jnp.where(mine, q, jnp.zeros_like(q))
            back_h = jnp.where(mine, back, jnp.zeros_like(back))
            delta = jnp.sum(jnp.where(mine, product, 0.0), axis=1, keepdims=True)
            low = probs[h, at, :keys]
            p = low.astype(f32)
            d_p = mm(back_h, value[:keys, :], NT)
            d_s = (p * (d_p - delta)).astype(bf16)
            result = jnp.where(mine, mm(d_s, key[:keys, :]), result)
            d_key[:keys, :] += mm(d_s, q_h, TN)
            d_value[:keys, :] += mm(low, back_h, TN)
        d_query[at, :] = result
    for b in range(length // step):
        at = pl.ds(b * step, step)
        c, s = cosine[at, :], sine[at, :]
        d_qkv[at, :cols] = turned(d_query[at, :] * scale, c, -s).astype(bf16)
        d_qkv[at, cols : 2 * cols] = turned(d_key[at, :] * scale, c, -s).astype(bf16)
        d_qkv[at, 2 * cols :] = d_value[at, :].astype(bf16)


def qkv_back(
    sizes, meta, g_all, weights, d_qkv, first_in, normed, vecs, part, sums, own24, pick24, own96, pick96,
    part_near, part_far, grads, place, base,
):
    f32, bf16 = jnp.float32, jnp.bfloat16
    nd, nc, per_d, held, nb, rows = sizes
    length, width = g_all.shape
    block = length // nc
    cols = held * HD
    ff = own96.shape[1]
    total = nd * nc
    w_qkv = weights[:, : 3 * cols]
    g_one = vecs[0:1, :]
    qkv_sum = jnp.zeros((1, 3 * cols), f32)
    gain_sum = jnp.zeros((1, width), f32)
    shift_sum = jnp.zeros((1, width), f32)
    for i in range(nc):
        half = part_near if i < nc // 2 else part_far
        at = pl.ds(pl.multiple_of(meta[i] * block, block), block)
        dq = d_qkv[at, :]
        qkv_sum += jnp.sum(dq.astype(f32), axis=0, keepdims=True)
        first = mm(dq, w_qkv, NT)
        gain_sum += jnp.sum(first * normed[at, :].astype(f32), axis=0, keepdims=True)
        shift_sum += jnp.sum(first, axis=0, keepdims=True)
        half[i % (nc // 2)] = (first * g_one + part[at, :].astype(f32)).astype(bf16)
    grad_qkv = mm(first_in[...], d_qkv[...], TN).astype(bf16)
    rows_d = width // nd
    for d in range(nd):
        grads[place(d), base : base + rows_d, :] = grad_qkv[d * rows_d : (d + 1) * rows_d]
    own = g_all[pl.ds(pl.multiple_of(meta[0] * block, block), block), :].astype(f32)
    own_sum = jnp.sum(own, axis=0, keepdims=True)

    def halves(row):
        high = row.astype(bf16).astype(f32)
        return high, row - high

    kept = iota((total, width), 0) == own24[...]
    up_owner = iota((total, ff), 0) == own96[...] * nc + meta[10]
    col_owner, col_place = column_places(meta, nb, cols, width, per_d, held)
    col_pick = (iota((block, 3 * cols), 0) == col_place).astype(f32).astype(bf16)
    col_kept = iota((total, 3 * cols), 0) == col_owner
    line = iota((total, 8, block), 1)
    packed = [jnp.zeros((total, 8, block), f32)] * 3
    entries = [
        (qkv_sum * meta[11].astype(f32), col_kept, col_pick),
        (sums[2:3, :ff], up_owner, pick96[...]),
        (own_sum, kept, pick24[...]),
        (gain_sum, kept, pick24[...]),
        (shift_sum, kept, pick24[...]),
        (sums[0:1, :], kept, pick24[...]),
        (sums[1:2, :], kept, pick24[...]),
    ]
    for k, (vector, where, pick) in enumerate(entries):
        for n, piece in enumerate(halves(vector)):
            spread = mm(jnp.where(where, piece, 0.0).astype(bf16), pick, NT)
            number = k + 8 * n
            packed[number % 3] = jnp.where(line == number // 3, spread[:, None, :], packed[number % 3])
    vector_rows = jnp.concatenate(packed, axis=2).reshape(nd, nc * 8, 3 * block).astype(bf16)
    for d in range(nd):
        grads[place(d), base + rows_d :, :] = vector_rows[d]


def backward_kernel(
    sizes, meta, near, far, weights, w_out, down, cosine, sine, query, key, value, attended, probs, hidden, slope,
    first_in, second_in, normed, vecs, own24, pick24, own96, pick96,
    keep, give, part_near, part_far,
    g_all, part, sums, pre_grad, d_qkv, d_query, d_key, d_value, grads,
):
    nd, nc, rows = sizes[0], sizes[1], sizes[5]
    base = nc * rows + 2 * (down.shape[0] // nd) + 2 * HD

    def place(d):
        other = meta[12] ^ d
        return (other >> 1) + (other & 1) * 2

    mlp_back(
        sizes, meta, near, far, weights, down, attended, hidden, slope, second_in, normed, vecs, part, g_all, sums, pre_grad,
        grads, place,
    )
    attention_back(
        sizes, meta, g_all, w_out, cosine, sine, query, key, value, attended, probs, d_qkv, d_query, d_key, d_value
    )
    qkv_back(
        sizes, meta, g_all, weights, d_qkv, first_in, normed, vecs, part, sums, own24, pick24, own96, pick96,
        part_near, part_far, grads, place, base,
    )
    keep[...] = grads[:2]
    give[...] = grads[2:]


def unpack_kernel(per_d, nd, units, rows, back, grad_qkv, grad_up, *vectors):
    f32 = jnp.float32
    nc = back.shape[0]
    held = nd // 2
    width = grad_qkv.shape[1] // 3
    cols = held * HD
    pieces = [None] * (3 * per_d * nd)
    ups = [None] * (nd * nc)
    total = jnp.zeros((8, 3 * 128), f32)
    for t in range(nc):
        group, half = HEAD_OF[t // 2], t % 2
        w = back[t].astype(f32)
        if group is not None:
            for part in range(3):
                for k in range(held):
                    at = part * cols + k * HD
                    pieces[part * per_d * nd + per_d * (held * half + k) + group] = w[rows : 2 * rows, at : at + HD]
        total = total + w[2 * rows :]
        for k in range(nd):
            ups[k * nc + t] = w[:rows, k * units : (k + 1) * units]
    grad_qkv[...] = jnp.concatenate(pieces, axis=1)
    grad_up[...] = jnp.concatenate(ups, axis=1)

    def kind(k):
        return total[k // 3 : k // 3 + 1, 128 * (k % 3) : 128 * (k % 3) + 128]

    for k, vector in enumerate(vectors):
        vector[...] = (kind(k) + kind(k + 8))[:, : vector.shape[1]]


def device_table(nd, nc):
    table = []
    for d in range(nd):
        for c in range(nc):
            group = HEAD_OF[c // 2]
            spare = c ^ 1 ^ (6 if c // 2 == 1 else 2)
            table.append([c ^ k for k in slot_order(nc)] + [c % 2, group or 0, c, int(group is not None), d, spare])
    return np.asarray(table, np.int32)


def final_kernel(inner, tokens, cotangent, m1, m2, m3, out):
    f32 = jnp.float32
    x = tokens[...].astype(f32)
    centered = x - jnp.mean(x, axis=1, keepdims=True)
    inverse = lax.rsqrt(jnp.mean(centered * centered, axis=1, keepdims=True) + eps)
    normed = centered * inverse
    n = inner[...] + m1[...].astype(f32) + m2[...].astype(f32) + m3[...].astype(f32)
    n = n - jnp.mean(n, axis=1, keepdims=True) - normed * jnp.mean(n * normed, axis=1, keepdims=True)
    out[...] = (cotangent[...].astype(f32) + n * inverse).astype(out.dtype)


def head_split_plan(
    tokens,
    segment_numbers,
    cotangent,
    query_key_value_weight,
    query_key_value_bias,
    output_matrix,
    output_bias,
    up_matrix,
    up_input_bias,
    down_matrix,
    down_output_bias,
    first_gain,
    first_shift,
    second_gain,
    second_shift,
):
    f32, bf16, i32 = jnp.float32, jnp.bfloat16, jnp.int32
    nd, nc = lax.axis_size("dp"), lax.axis_size("ctx")
    block, width = tokens.shape[1], tokens.shape[2]
    per_d = width // HD // nd
    held = nd // 2
    cols = held * HD
    rows = query_key_value_weight.shape[0]
    units = down_matrix.shape[0]
    ff = nd * units
    nb, nu = query_key_value_bias.shape[0], up_input_bias.shape[0]
    length = nc * block
    rows_d = nc * rows
    sizes = (nd, nc, per_d, held, nb, rows)
    d, c = lax.axis_index("dp"), lax.axis_index("ctx")
    pair_index, half = c // 2, c % 2
    group = jnp.where(pair_index == 3, 2, jnp.minimum(pair_index, 1))
    active = pair_index != 2
    lane = np.arange(width)
    own24 = jnp.asarray((lane // rows)[None], i32)
    pick24 = jnp.asarray(np.arange(block)[:, None] == lane[None] % rows, bf16)
    unit = np.arange(ff)
    own96 = jnp.asarray((unit // units)[None], i32)
    pick96 = jnp.asarray(np.arange(block)[:, None] == unit[None] % units, bf16)
    freq = jnp.asarray((10000.0 ** (-np.arange(ROT // 2) * 2.0 / ROT))[:, None], f32)

    vectors = [
        query_key_value_bias, up_input_bias, output_bias, down_output_bias, first_gain, first_shift, second_gain,
        second_shift, segment_numbers,
    ]
    lanes = 3 * cols + ff + block
    bits = list(range(2, nc, 2))
    target = active & ((d < nd // 2) == (half == 0))
    meta = jnp.asarray(device_table(nd, nc), i32)
    meta = lax.dynamic_index_in_dim(meta, d * nc + c, 0, False)
    payload = lambda count: like((count, rows, lanes), bf16)
    mine, to_two, to_four, to_six, _ = call(
        partial(message_kernel, per_d, nd, nc, units),
        [payload(3), payload(3), payload(2), payload(3), payload(nc)],
        [meta, query_key_value_weight, up_matrix, output_matrix] + [v.reshape(1, -1) for v in vectors],
        limit=VMEM_MOST,
    )
    two, four, six = swapped(to_two, 2), swapped(to_four, 4), swapped(to_six, 6)
    copies = (nc // 2, block, width)
    x_near = pair_exchange(jnp.broadcast_to(after(tokens, two), copies))
    g_own = after(cotangent[0], x_near)
    g_moved = [swapped(g_own, bit) for bit in bits]
    g_near = jnp.stack([g_own] + g_moved)
    message_far = swapped(
        jnp.stack([mine[1], two[1], four[1], six[1], mine[2], jnp.where(pair_index == 1, six[2], two[2])]), 1
    )
    (package,) = call(
        package_kernel,
        [like((rows_d + units + HD, lanes), bf16)],
        [meta, mine, two, four, six, message_far, down_matrix],
        scratch=[pltpu.VMEM((nc, rows, lanes), f32)] * 2,
        limit=VMEM_MOST,
    )
    x_far = swapped(after(x_near, package), 1)
    g_far = swapped(after(g_near, x_far), 1)
    cosine, sine, begin = call(
        partial(tables_kernel, nc, rows), [like((length, cols), f32)] * 3, [package, freq], smem=False
    )
    across = swapped_dp(package, 2)
    own_pair = jnp.stack([package, after(across, cosine, x_far, *g_moved)])
    other_pair = swapped_dp(own_pair, 1)

    full = lambda dtype: like((length, width), dtype)
    part_shape = like((nc // 2, block, width), bf16)
    (
        out_near, out_near_own, out_far, out_far_own, first_in, second_in, normed, query, key, value, attended, probs, hidden, slope, vecs, weights,
        w_out, w_down,
    ) = call(
        partial(forward_kernel, sizes),
        [like((nc // 2 - 1, block, width), bf16), like((block, width), bf16)] * 2 + [full(bf16)] * 3
        + [like((length, cols), bf16)] * 3
        + [like((length, cols), f32), like((held, length, length), bf16)]
        + [like((length, ff), bf16)] * 2
        + [like((8, width), f32), like((width, 3 * cols + ff), bf16), like((cols, width), bf16), like((ff, width), bf16)],
        [meta, x_near, x_far, own_pair, other_pair, cosine, sine, begin, own24, pick24, own96, pick96],
        scratch=[pltpu.VMEM((nd, rows_d, lanes), bf16), pltpu.VMEM((nd, HD, width), bf16)],
        flops=FORWARD_WORK,
    )
    half_rows = rows_d + 2 * units + 2 * HD
    grad_rows = half_rows + rows_d + 8 * nc
    keep, give, n_near, n_far = call(
        partial(backward_kernel, sizes),
        [like((nd // 2, grad_rows, 3 * cols), bf16)] * 2 + [part_shape, part_shape],
        [meta, g_near, g_far, weights, w_out, w_down, cosine, sine, query, key, value, attended, probs, hidden, slope,
         first_in, second_in, normed, vecs, own24, pick24, own96, pick96],
        scratch=[
            pltpu.VMEM((length, width), bf16),
            pltpu.VMEM((length, width), bf16),
            pltpu.VMEM((8, width), f32),
            pltpu.VMEM((length, ff), bf16),
            pltpu.VMEM((length, 3 * cols), bf16),
        ]
        + [pltpu.VMEM((length, cols), f32)] * 3
        + [pltpu.VMEM((nd, grad_rows, 3 * cols), bf16)],
        flops=BACKWARD_WORK,
    )

    def near_sum(near, far):
        total = near.astype(f32) + swapped(far, 1).astype(f32)
        return total, total.astype(bf16)

    out_low = near_sum(out_near, after(out_far, g_far))[1]
    n_far, give = lax.optimization_barrier((n_far, give, out_low))[:2]
    give_moved = swapped_dp(give, 1)
    grads = keep.astype(f32) + give_moved.astype(f32)
    grads_low = grads[1].astype(bf16)
    out_low = after(out_low, grads_low)
    out_moved = [swapped(out_low[k], bit) for k, bit in enumerate(bits)]
    grads_moved = swapped_dp(grads_low, 2)
    n_total, n_low = near_sum(after(n_near, out_moved[0]), n_far)
    n_low = after(n_low, out_moved[1], out_moved[2], grads_moved)
    n_moved = [swapped(n_low[1 + k], bit) for k, bit in enumerate(bits)]
    grads = grads[0] + grads_moved.astype(f32)
    at_out = rows_d + 2 * units
    at_qkv = at_out + 2 * HD
    at_vec = at_qkv + rows_d
    back = jnp.concatenate(
        [
            grads[:rows_d].reshape(nc, rows, ff),
            grads[at_qkv:at_vec].reshape(nc, rows, 3 * cols),
            grads[at_vec:].reshape(nc, 8, 3 * cols),
        ],
        axis=1,
    )
    back = lax.all_to_all(back.astype(bf16), "ctx", 0, 0, tiled=True)
    down_weight_grad = jnp.concatenate([grads[rows_d : rows_d + units], grads[rows_d + units : at_out]], axis=1)
    head_rows = jnp.concatenate([grads[at_out : at_out + HD], grads[at_out + HD : at_qkv]], axis=1).astype(bf16)
    head_rows = jnp.where(target, head_rows, jnp.zeros_like(head_rows))
    strip = lax.dynamic_update_slice(jnp.zeros((rows_d, width), bf16), head_rows, (HD * group, 0))
    out_sum = sum((m.astype(f32) for m in out_moved), out_near_own.astype(f32))
    strip = after(strip, n_moved[0], out_sum)

    def strip_block(index):
        return lax.dynamic_slice_in_dim(strip, index * rows, rows, 0)

    third = jnp.where(group == 0, 2, jnp.where(group == 1, 4, 5))
    both = swapped(jnp.concatenate([strip_block(c ^ 1), out_far_own], axis=0), 1)
    mixed_sum = out_sum + both[rows:].astype(f32)
    mixed = (tokens[0].astype(f32) + (mixed_sum + vecs[4])).astype(bf16)
    strips = [
        both[:rows],
        sent(strip_block(third), lambda k: [(0, 2), (2, 4), (6, 5)] if k < nd // 2 else [(1, 2), (3, 4), (7, 5)]),
        sent(strip_block(jnp.int32(5)), lambda k: [(2, 5)] if k < nd // 2 else [(3, 5)]),
    ]
    out_weight_grad = sum((m.astype(f32) for m in strips), strip_block(c).astype(f32))

    qkv_weight_grad, up_weight_grad, *small = call(
        partial(unpack_kernel, per_d, nd, units, rows),
        [like((rows, 3 * width), f32), like((rows, nc * ff), f32), like((1, nb), f32), like((1, nu), f32)]
        + [like((1, rows), f32)] * 5,
        [back],
        smem=False,
    )
    (tokens_grad,) = call(
        final_kernel,
        [like((block, width), bf16)],
        [after(n_total[0], small[0]), tokens[0], cotangent[0]] + n_moved,
        smem=False,
    )
    small = [v.reshape(-1) for v in small]
    return (
        mixed[None],
        tokens_grad[None],
        qkv_weight_grad,
        small[0],
        out_weight_grad,
        small[2],
        up_weight_grad,
        small[1],
        down_weight_grad,
        small[2],
        small[3],
        small[4],
        small[5],
        small[6],
    )


def head_split_fits(nd, nc, width):
    return nd % 2 == 0 and width // HD == 3 * nd and nc == 8 and width // (nd * nc) * 8 == 3 * HD


def per_device(tokens, *others):
    nd, nc = lax.axis_size("dp"), lax.axis_size("ctx")
    plan = head_split_plan if head_split_fits(nd, nc, tokens.shape[2]) else gathered_plan
    return plan(tokens, *others)


def solution(mesh):
    in_specs = (
        P("dp", "ctx", None),
        P("dp", "ctx"),
        P("dp", "ctx", None),
        P(("dp", "ctx"), None),
        P(("dp", "ctx")),
        P(("dp", "ctx"), None),
        P(("dp", "ctx")),
        P(("dp", "ctx"), None),
        P(("dp", "ctx")),
        P(("dp", "ctx"), None),
        P(("dp", "ctx")),
        P(("dp", "ctx")),
        P(("dp", "ctx")),
        P(("dp", "ctx")),
        P(("dp", "ctx")),
    )
    out_specs = (
        P("dp", "ctx", None),
        P("dp", "ctx", None),
        P(("dp", "ctx"), None),
        P(("dp", "ctx")),
        P(("dp", "ctx"), None),
        P(("dp", "ctx")),
        P(("dp", "ctx"), None),
        P(("dp", "ctx")),
        P(("dp", "ctx"), None),
        P(("dp", "ctx")),
        P(("dp", "ctx")),
        P(("dp", "ctx")),
        P(("dp", "ctx")),
        P(("dp", "ctx")),
    )
    return jax.shard_map(
        per_device, mesh=mesh, in_specs=in_specs, out_specs=out_specs, check_vma=False
    )
```
